512 devices in a mesh: ctx: 64 (over y_lo, z, core), head: 8 (over y_hi, x).
Axes of the slice: x: 4, y: 8 (y_hi: 2, y_lo: 4; y = y_hi * 4 + y_lo), z: 8, core: 2. Of those that a mesh axis runs over, the one named last changes fastest.
Arguments:
- span_query: bfloat16 [4096, 12288], P('ctx', 'head'), may hold values from -106 to 106
- span_latent: bfloat16 [4096, 576], P('ctx'), may hold values from -12.5 to 12.5
- cache_latent: bfloat16 [1024, 576], P('ctx'), may hold values from -6 to 6
- cache_length: int32 [1], replicated, may hold values from 512 to 1024
- kv_up_weight: bfloat16 [512, 16384], P(None, 'head'), may hold values from -0.25 to 0.25
- out_weight: bfloat16 [8192, 7168], P('head', 'ctx'), may hold values from -0.5 to 0.5
Outputs:
- mixed: bfloat16 [4096, 7168], P('head', 'ctx')
The draws below stay inside these ranges and needn't reach their ends.
All inputs are finite; a program needn't handle non-finite values.
Results may differ from the reference program's by a relative error of at most 0.019.
Values may be sent and summed in bfloat16 or wider, within the bound.
A program may use at most 64 MiB of HBM per device.

```python
import math
import jax
import jax.numpy as jnp
from jax import lax

D = 7168
LATENT = 512
ROPE = 64
NOPE = 128
VDIM = 128
H = 64
SPAN = 4096
CACHE = 1024
N_HEAD = 8


def rope_base(key):
    return jax.random.truncated_normal(key, -6.0, 6.0, (SPAN, ROPE), jnp.float32)


def draw_span_latent(key, part):
    shared = rope_base(key)
    key = jax.random.fold_in(key, 11)
    latent = jax.random.truncated_normal(key, -6.0, 6.0, (SPAN, LATENT), jnp.float32)
    rope_part = shared
    return jnp.concatenate([latent, rope_part], axis=1).astype(jnp.bfloat16)


def draw_span_query(key, part):
    key = jax.random.fold_in(key, 7)
    values = jax.random.truncated_normal(key, -6.0, 6.0, (SPAN, H, NOPE + ROPE), jnp.float32)
    return values.reshape(SPAN, H * (NOPE + ROPE)).astype(jnp.bfloat16)


def steps_of(rng, extent, cuts, least, top_value):
    level = 1.0
    for axis_at, parts in cuts:
        draws = jax.random.uniform(jax.random.fold_in(jax.random.fold_in(rng, 6), axis_at), (parts,), jnp.float32, least / len(cuts), top_value / len(cuts))
        level = level * jnp.repeat(jnp.exp(draws), extent[axis_at] // parts).reshape((-1,) + (1,) * (len(extent) - 1 - axis_at))
    return level


def gaussian(key, dims, width, reach, shards=(), held_as=jnp.bfloat16):
    gain = steps_of(key, dims, shards, -0.22, 0.18) if shards else 1.0
    drawn = jax.random.normal(key, dims, jnp.float32) * width * gain
    return jnp.minimum(jnp.maximum(drawn, -reach), reach).astype(held_as)


def setup_inputs(seed: int = 0) -> dict:
    streams_of = jax.random.split(jax.random.key(seed), 7)
    return {
        "span_query": draw_span_query(jax.random.fold_in(streams_of[6], 71), 0),
        "span_latent": draw_span_latent(jax.random.fold_in(streams_of[6], 71), 0),
        "cache_latent": gaussian(streams_of[2], (CACHE, LATENT + ROPE), 1.0, 6.0, ((0, 64),)),
        "cache_length": jax.random.randint(streams_of[3], (1,), CACHE // 2, CACHE + 1).astype(jnp.int32),
        "kv_up_weight": gaussian(streams_of[4], (LATENT, H * (NOPE + VDIM)), LATENT ** -0.5, 0.25, ((1, 8),)),
        "out_weight": gaussian(streams_of[5], (H * VDIM, D), (H * VDIM // 64) ** -0.5, 0.5, ((0, 8), (1, 64))),
    }


mscale_factor = (1.0 + 0.1 * math.log(40.0)) ** 2

def reference(span_query, span_latent, cache_latent, cache_length, kv_up_weight, out_weight):
    score_scale = mscale_factor / math.sqrt(NOPE + ROPE)
    shaped = span_query.reshape(SPAN, H, NOPE + ROPE)
    kv_shaped = kv_up_weight.reshape(LATENT, H, NOPE + VDIM)
    absorbed = jnp.einsum('thn,chn->thc', shaped[:, :, :NOPE].astype(jnp.float32), kv_shaped[:, :, :NOPE].astype(jnp.float32)).astype(jnp.bfloat16)
    queries = jnp.concatenate([absorbed, shaped[:, :, NOPE:]], axis=2)
    all_keys = jnp.concatenate([cache_latent, span_latent], axis=0).astype(jnp.float32)
    key_index = jnp.arange(CACHE + SPAN, dtype=jnp.int32)
    token_index = jnp.arange(SPAN, dtype=jnp.int32)
    allowed = jnp.where(key_index[None, :] < CACHE, key_index[None, :] < cache_length[0], key_index[None, :] - CACHE <= token_index[:, None])

    def per_head(operands):
        head_queries, up_value = operands
        scores = jnp.dot(head_queries.astype(jnp.float32), all_keys.T) * score_scale
        scores = jnp.where(allowed, scores, -jnp.inf)
        row_max = lax.optimization_barrier(jnp.max(scores, axis=1, keepdims=True))
        weights = jnp.where(allowed, jnp.exp(scores - row_max), 0.0)
        totals = lax.optimization_barrier(jnp.sum(weights, axis=1, keepdims=True))
        rounded = lax.optimization_barrier(weights.astype(jnp.bfloat16))
        latent_out = (jnp.dot(rounded.astype(jnp.float32), all_keys[:, :LATENT]) / totals).astype(jnp.bfloat16)
        return jnp.dot(latent_out, up_value, preferred_element_type=jnp.float32).astype(jnp.bfloat16)
    heads_out = lax.map(per_head, (jnp.transpose(queries, (1, 0, 2)), jnp.transpose(kv_shaped[:, :, NOPE:], (1, 0, 2))))
    attended = jnp.transpose(heads_out, (1, 0, 2)).reshape(SPAN, H * VDIM)
    group_width = H // N_HEAD * VDIM
    grouped_out = jnp.transpose(attended.reshape(SPAN, N_HEAD, group_width), (1, 0, 2))
    grouped_weight = out_weight.reshape(N_HEAD, group_width, D)

    def add_group(running, operands):
        part_rows, part_weight = operands
        partial_value = jnp.dot(part_rows, part_weight, preferred_element_type=jnp.float32).astype(jnp.bfloat16)
        partial_value = lax.optimization_barrier(partial_value)
        return (running + partial_value.astype(jnp.float32), None)
    summed, unused = lax.scan(add_group, jnp.zeros((SPAN, D), jnp.float32), (grouped_out, grouped_weight))
    return summed.astype(jnp.bfloat16)
```

```python
import math

import jax
import jax.numpy as jnp
from jax import lax
from jax.experimental import pallas as pl
from jax.experimental.pallas import tpu as pltpu
from jax.sharding import PartitionSpec as P

LATENT = 512
ROPE = 64
NOPE = 128
VDIM = 128
HEADS = 8
TOK = 64
CROWS = 16
SHARD = TOK + CROWS
WIDE = 640
HALF = 4 * SHARD
BLOCK = 2 * HALF
COLS = 112
ROWS = HEADS * TOK
CHUNK = 256
MASKED = -1e30
FAR = 1 << 30
MESH = pl.DeviceIdType.MESH
SCALE2 = (1.0 + 0.1 * math.log(40.0)) ** 2 / math.sqrt(NOPE + ROPE) * math.log2(math.e)


def kernel(
    query_ref,
    span_ref,
    cache_ref,
    length_ref,
    kv_ref,
    w_ref,
    out_ref,
    keys,
    mine,
    queries,
    maxima,
    totals,
    acc,
    latent_out,
    wbuf,
    att,
    part,
    landed,
    reduced,
    final,
    s_pre,
    s_ring,
    s_leaf,
    s_sib,
    s_w,
    s_wsib,
    s_att,
    s_x,
    s_f,
    r_ring,
    r_leaf,
    r_sib,
    r_w,
    r_att,
    r_x,
    r_f,
):
    ctx = lax.axis_index("ctx")
    head = lax.axis_index("head")
    x, yh = head % 4, head // 4
    q, z, c = ctx // 16, (ctx // 2) % 8, ctx % 2
    y = yh * 4 + q

    def device(dx, dy, dz, dc):
        return {"ctx": ((dy % 4) * 8 + dz) * 2 + dc, "head": (dy // 4) * 4 + dx}

    z_up = device(x, y, (z + 1) % 8, c)
    z_down = device(x, y, (z + 7) % 8, c)
    sibling = device(x, y, z, 1 - c)
    lead = jnp.where(c == 0, x, q)
    two = jnp.where(q % 2 == 0, 2, 6)

    def leaf(delta):
        step = two if delta == 2 else (delta if delta == 1 else 7)
        return device(
            jnp.where(c == 0, (x + delta) % 4, x), jnp.where(c == 0, y, (y + step) % 8), z, c
        )

    x0 = 2 * (q % 2)
    role = (x - x0 + 4) % 4
    my_j = jnp.where((role == 1) | (role == 2), 1, 0)
    my_pair = role // 2

    def target(b):
        return x0 + my_j, 4 * (q // 2) + 2 * my_pair + b // 2, b % 2

    def is_me(dx, dy, dc):
        return (dx == x) & (dy == y) & (dc == c)

    def copy(src, dst, ssem, rsem, dev):
        return pltpu.make_async_remote_copy(
            src_ref=src, dst_ref=dst, send_sem=ssem, recv_sem=rsem, device_id=dev, device_id_type=MESH
        )

    barrier = pltpu.get_barrier_semaphore()

    def greet(dev):
        pl.semaphore_signal(barrier, inc=1, device_id=dev, device_id_type=MESH)

    greet(z_up)
    greet(z_down)
    greet(sibling)
    for d in (1, 2, 3):
        greet(device((x + d) % 4, y, z, c))
        greet(device(x, yh * 4 + (q + d) % 4, z, c))
    for d in (1, 2, 6, 7):
        greet(device(x, (y + d) % 8, z, c))
    src_q = 2 * yh + x // 2
    src_j = x % 2
    src_x = jnp.where(q // 2 == 0, x, (2 * (x // 2) + 3 - src_j) % 4)
    for b in range(4):
        sx, sy, sc = src_x, src_q + 4 * (b // 2), b % 2

        @pl.when(jnp.logical_not(is_me(sx, sy, sc)))
        def _():
            greet(device(sx, sy, z, sc))

    selfs = 0
    for b in range(4):
        selfs = selfs + jnp.where(is_me(*target(b)), 1, 0)

    mine[:CROWS, :LATENT] = cache_ref[:, :LATENT]
    mine[CROWS:, :LATENT] = span_ref[:, :LATENT]
    mine[:CROWS, LATENT:] = jnp.concatenate(
        [cache_ref[:, LATENT:], jnp.zeros((CROWS, 64), jnp.bfloat16)], axis=1
    )
    mine[CROWS:, LATENT:] = jnp.concatenate(
        [span_ref[:, LATENT:], jnp.zeros((TOK, 64), jnp.bfloat16)], axis=1
    )

    def slot(zp, qp):
        return keys.at[zp, pl.ds(pl.multiple_of(c * HALF + qp * SHARD, SHARD), SHARD)]

    has_primary = (c == 1) | (q == x)

    @pl.when(has_primary)
    def _():
        slot(z, lead)[...] = mine[...]

    pl.semaphore_wait(barrier, 2 + 1 + 3 + 3 + 4 + 4 - selfs)

    def at(k):
        return (z + 8 + jnp.where(k % 2 == 1, -((k + 1) // 2), k // 2)) % 8

    def pre(n):
        d = (1, 2, 7)[n]
        return copy(mine, slot(z, x), s_pre.at[n], r_ring.at[z], device(x, (y + d) % 8, z, c))

    sends_pre = (c == 0) & (q == x)

    @pl.when(sends_pre)
    def _():
        for n in range(3):
            pre(n).start()

    @pl.when(jnp.logical_not(has_primary))
    def _():
        pre(0).wait_recv()

    def ring_copy(buf, zp, sem, ssem, dev):
        return copy(buf, buf, ssem.at[sem], r_ring.at[zp], dev)

    def stage1(k):
        zp = at(k)
        piece = slot(zp, lead)
        up = ring_copy(piece, zp, k, s_ring, z_up)
        down = ring_copy(piece, zp, k, s_ring, z_down)
        first_down = ring_copy(piece, zp, 8, s_ring, z_down)

        @pl.when(k > 0)
        def _():
            up.wait_recv()

        @pl.when((k == 0) | ((k % 2 == 1) & (k < 7)))
        def _():
            up.start()

        @pl.when((k % 2 == 0) & (k > 0) & (k < 6))
        def _():
            down.start()

        @pl.when(k == 0)
        def _():
            first_down.start()

        for n, d in enumerate((1, 3, 2)):
            copy(piece, piece, s_leaf.at[3 * k + n], r_leaf.at[zp * 4 + lead], leaf(d)).start()

    def half(zp, core):
        return keys.at[zp, pl.ds(pl.multiple_of(core * HALF, HALF), HALF)]

    def sib_copy(k):
        zp = at(k)
        return copy(half(zp, c), half(zp, c), s_sib.at[k], r_sib.at[zp], sibling)

    def stage2(k):
        zp = at(k)
        for d in (1, 3, 2):
            qp = (lead + d) % 4
            copy(slot(zp, qp), slot(zp, qp), s_leaf.at[0], r_leaf.at[zp * 4 + qp], leaf(1)).wait_recv()
        sib_copy(k).start()

    place = lax.broadcasted_iota(jnp.int32, (1, BLOCK), 1)
    core_of = jnp.where(place >= HALF, 1, 0)
    within = place - core_of * HALF
    plane = sum(jnp.where(within >= n * SHARD, 1, 0) for n in (1, 2, 3))
    row = within - plane * SHARD
    token_base = plane * 1024 + core_of * TOK + row - CROWS
    cache_base = plane * 256 + core_of * CROWS + row
    cached = row < CROWS
    length = length_ref[0]

    def flash(zp):
        code = jnp.where(
            cached,
            jnp.where(cache_base + zp * 32 < length, -1, FAR),
            token_base + zp * 128,
        )

        def chunk(i, carry):
            rows = pl.ds(pl.multiple_of(i * CHUNK, CHUNK), CHUNK)
            block = keys[zp]
            token = ctx * TOK + lax.broadcasted_iota(jnp.int32, (CHUNK, 1), 0) % TOK
            scores = lax.dot_general(
                queries[rows], block, (((1,), (1,)), ((), ())), preferred_element_type=jnp.float32
            )
            scores = jnp.where(code <= token, scores * SCALE2, MASKED)
            before = maxima[rows, :1]
            raised = jnp.maximum(before, jnp.max(scores, axis=1, keepdims=True))
            weights = jnp.exp2(scores - raised)
            factor = jnp.exp2(before - raised)
            maxima[rows] = jnp.broadcast_to(raised, (CHUNK, 128))
            totals[rows] = totals[rows] * factor + jnp.sum(weights, axis=1, keepdims=True)
            acc[rows] = acc[rows] * factor + jnp.dot(
                weights.astype(jnp.bfloat16), block[:, :LATENT], preferred_element_type=jnp.float32
            )
            return carry

        lax.fori_loop(0, ROWS // CHUNK, chunk, 0)

    stage1(0)

    for h in range(HEADS):
        nope = query_ref[:, h * 192 : h * 192 + NOPE]
        rope = query_ref[:, h * 192 + NOPE : (h + 1) * 192]
        absorbed = lax.dot_general(
            nope,
            kv_ref[:, h * 256 : h * 256 + NOPE],
            (((1,), (1,)), ((), ())),
            preferred_element_type=jnp.float32,
        ).astype(jnp.bfloat16)
        queries[h * TOK : (h + 1) * TOK, :LATENT] = absorbed
        queries[h * TOK : (h + 1) * TOK, LATENT:] = jnp.concatenate(
            [rope, jnp.zeros((TOK, 64), jnp.bfloat16)], axis=1
        )
    maxima[...] = jnp.full((ROWS, 128), MASKED, jnp.float32)
    totals[...] = jnp.zeros((ROWS, 128), jnp.float32)
    acc[...] = jnp.zeros((ROWS, LATENT), jnp.float32)

    def w_lanes(qp, core):
        return wbuf.at[:, pl.ds(pl.multiple_of(qp * 256 + core * 128, 128), 128)]

    w_lanes(q, c)[...] = jnp.concatenate(
        [w_ref[...], jnp.zeros((1024, 128 - COLS), jnp.bfloat16)], axis=1
    )

    stage1(1)
    stage1(2)

    def body(i, carry):
        for n in (3, 4):

            @pl.when(2 * i + n < 8)
            def _():
                stage1(2 * i + n)

        @pl.when(i < 8)
        def _():
            stage2(i)

        @pl.when(i > 0)
        def _():
            sib_copy(i - 1).wait_recv()
            flash(at(i - 1))

        return carry

    lax.fori_loop(0, 3, body, 0)

    def w_copy(d):
        return copy(
            w_lanes(q, c), w_lanes(q, c), s_w.at[d - 1], r_w.at[q * 2 + c], device(x, yh * 4 + (q + d) % 4, z, c)
        )

    for d in (1, 2, 3):
        w_copy(d).start()

    lax.fori_loop(3, 9, body, 0)

    latent_out[...] = (acc[...] / totals[:, :1]).astype(jnp.bfloat16)
    for h in range(HEADS):
        att[z, :, h * VDIM : (h + 1) * VDIM] = jnp.dot(
            latent_out[h * TOK : (h + 1) * TOK],
            kv_ref[:, h * 256 + NOPE : (h + 1) * 256],
            preferred_element_type=jnp.float32,
        ).astype(jnp.bfloat16)

    def att_copy(zp, n, dev):
        return copy(att.at[zp], att.at[zp], s_att.at[n], r_att.at[zp], dev)

    att_copy(z, 0, z_up).start()
    att_copy(z, 7, z_down).start()

    def w_sib(qp):
        return copy(w_lanes(qp, c), w_lanes(qp, c), s_wsib.at[qp], r_w.at[qp * 2 + c], sibling)

    for d in (1, 2, 3):
        qp = (q + d) % 4
        copy(w_lanes(qp, c), w_lanes(qp, c), s_w.at[0], r_w.at[qp * 2 + c], sibling).wait_recv()
    for qp in range(4):
        w_sib(qp).start()
    for qp in range(4):
        copy(w_lanes(qp, 1 - c), w_lanes(qp, 1 - c), s_w.at[0], r_w.at[qp * 2 + 1 - c], sibling).wait_recv()

    def collector(zp, pair):
        j = zp // 4
        return (x0 + jnp.where(pair == 0, j, 3 - j)) % 4

    def x_copy(zp, pair):
        r = collector(zp, pair)
        return r, copy(
            part.at[zp, :, pl.ds(pair * 512, 512)],
            landed.at[x, zp % 4],
            s_x.at[zp * 2 + pair],
            r_x.at[x * 4 + zp % 4],
            device(r, y, z, c),
        )

    def project(zp):
        part[zp] = jnp.dot(att[zp], wbuf[...], preferred_element_type=jnp.float32).astype(jnp.bfloat16)
        for pair in (0, 1):
            r, cp = x_copy(zp, pair)

            @pl.when(r != x)
            def _():
                cp.start()

    def out_step(k, carry):
        zp = at(k)

        @pl.when(k > 0)
        def _():
            att_copy(zp, k, z_up).wait_recv()

        @pl.when((k % 2 == 1) & (k < 7))
        def _():
            att_copy(zp, k, z_up).start()

        @pl.when((k % 2 == 0) & (k > 0) & (k < 6))
        def _():
            att_copy(zp, k, z_down).start()

        project(zp)
        return carry

    lax.fori_loop(0, 8, out_step, 0)

    def reduce_step(k, carry):
        zp = at(k)
        zi = zp % 4

        @pl.when(zp // 4 == my_j)
        def _():
            lanes = pl.ds(pl.multiple_of(my_pair * 512, 512), 512)
            total = part[zp, :, lanes].astype(jnp.float32)
            for d in (1, 2, 3):
                xs = (x + d) % 4
                copy(landed.at[xs, zi], landed.at[xs, zi], s_x.at[0], r_x.at[xs * 4 + zi], sibling).wait_recv()
                total = total + landed[xs, zi].astype(jnp.float32)
            reduced[pl.ds(pl.multiple_of(zi * TOK, TOK), TOK)] = total.astype(jnp.bfloat16)

        return carry

    lax.fori_loop(0, 8, reduce_step, 0)

    me_slot = yh * 2 + c
    for b in range(4):
        dx, dy, dc = target(b)
        src = reduced.at[:, pl.ds(b * 128, 128)]
        dst = final.at[me_slot]

        @pl.when(is_me(dx, dy, dc))
        def _():
            pltpu.make_async_copy(src, dst, r_f.at[me_slot]).start()

        @pl.when(jnp.logical_not(is_me(dx, dy, dc)))
        def _():
            copy(src, dst, s_f.at[b], r_f.at[me_slot], device(dx, dy, z, dc)).start()

    for core in range(2):
        for h in range(2):
            n = h * 2 + core
            copy(final.at[n], final.at[n], s_f.at[0], r_f.at[n], sibling).wait_recv()
        total = final[core].astype(jnp.float32) + final[2 + core].astype(jnp.float32)
        total = total[:, :COLS].astype(jnp.bfloat16)
        for zi in range(4):
            out_ref[zi * 128 + core * TOK : zi * 128 + (core + 1) * TOK] = total[zi * TOK : (zi + 1) * TOK]

    @pl.when(sends_pre)
    def _():
        for n in range(3):
            pre(n).wait_send()

    piece = slot(z, lead)
    for k in (0, 1, 2, 3, 4, 5, 8):
        copy(piece, piece, s_ring.at[k], r_ring.at[z], z_up).wait_send()
    for k in range(24):
        copy(piece, piece, s_leaf.at[k], r_ring.at[z], z_up).wait_send()
    for k in range(8):
        sib_copy(k).wait_send()
    for d in (1, 2, 3):
        w_copy(d).wait_send()
    for qp in range(4):
        w_sib(qp).wait_send()
    for n in (0, 1, 2, 3, 4, 5, 7):
        att_copy(z, n, z_up).wait_send()
    for zp in range(8):
        for pair in (0, 1):
            r, cp = x_copy(zp, pair)

            @pl.when(r != x)
            def _():
                cp.wait_send()

    for b in range(4):
        dx, dy, dc = target(b)

        @pl.when(jnp.logical_not(is_me(dx, dy, dc)))
        def _():
            copy(
                reduced.at[:, pl.ds(b * 128, 128)], final.at[me_slot], s_f.at[b], r_f.at[me_slot], sibling
            ).wait_send()


def on_device(span_query, span_latent, cache_latent, cache_length, kv_up_weight, out_weight):
    vmem = pl.BlockSpec(memory_space=pltpu.VMEM)
    dma = pltpu.SemaphoreType.DMA
    return pl.pallas_call(
        kernel,
        out_shape=jax.ShapeDtypeStruct((512, COLS), jnp.bfloat16),
        in_specs=[vmem, vmem, vmem, pl.BlockSpec(memory_space=pltpu.SMEM), vmem, vmem],
        out_specs=vmem,
        scratch_shapes=[
            pltpu.VMEM((8, BLOCK, WIDE), jnp.bfloat16),
            pltpu.VMEM((SHARD, WIDE), jnp.bfloat16),
            pltpu.VMEM((ROWS, WIDE), jnp.bfloat16),
            pltpu.VMEM((ROWS, 128), jnp.float32),
            pltpu.VMEM((ROWS, 128), jnp.float32),
            pltpu.VMEM((ROWS, LATENT), jnp.float32),
            pltpu.VMEM((ROWS, LATENT), jnp.bfloat16),
            pltpu.VMEM((1024, 1024), jnp.bfloat16),
            pltpu.VMEM((8, TOK, 1024), jnp.bfloat16),
            pltpu.VMEM((8, TOK, 1024), jnp.bfloat16),
            pltpu.VMEM((4, 4, TOK, 512), jnp.bfloat16),
            pltpu.VMEM((4 * TOK, 512), jnp.bfloat16),
            pltpu.VMEM((4, 4 * TOK, 128), jnp.bfloat16),
            dma((3,)),
            dma((9,)),
            dma((24,)),
            dma((8,)),
            dma((3,)),
            dma((4,)),
            dma((8,)),
            dma((16,)),
            dma((4,)),
            dma((8,)),
            dma((32,)),
            dma((8,)),
            dma((8,)),
            dma((8,)),
            dma((16,)),
            dma((4,)),
        ],
        compiler_params=pltpu.CompilerParams(
            collective_id=0, has_side_effects=True, vmem_limit_bytes=48 << 20
        ),
        cost_estimate=pl.CostEstimate(
            flops=8_000_000_000, bytes_accessed=4_000_000, transcendentals=2_600_000
        ),
        name="mla_prefill",
    )(span_query, span_latent, cache_latent, cache_length, kv_up_weight, out_weight)


def solution(mesh):
    return jax.shard_map(
        on_device,
        mesh=mesh,
        in_specs=(
            P("ctx", "head"),
            P("ctx", None),
            P("ctx", None),
            P(),
            P(None, "head"),
            P("head", "ctx"),
        ),
        out_specs=P("head", "ctx"),
        check_vma=False,
    )
```

```python
import math

import jax
import jax.numpy as jnp
from jax import lax
from jax.experimental import pallas as pl
from jax.experimental.pallas import tpu as pltpu
from jax.sharding import PartitionSpec as P

LATENT = 512
ROPE = 64
NOPE = 128
VDIM = 128
HEADS = 8
TOK = 64
CROWS = 16
SHARD = TOK + CROWS
WIDE = 640
HALF = 4 * SHARD
BLOCK = 2 * HALF
COLS = 112
ROWS = HEADS * TOK
MASKED = -1e30
FAR = 1 << 30
MESH = pl.DeviceIdType.MESH
SCALE2 = (1.0 + 0.1 * math.log(40.0)) ** 2 / math.sqrt(NOPE + ROPE) * math.log2(math.e)


def kernel(
    query_hbm,
    span_hbm,
    cache_hbm,
    length_ref,
    kv_hbm,
    w_hbm,
    out_ref,
    query_ref,
    span_ref,
    cache_ref,
    kv_ref,
    keys,
    mine,
    queries,
    maxima,
    totals,
    acc,
    latent_out,
    wbuf,
    att,
    part,
    landed,
    reduced,
    final,
    s_in,
    s_pre,
    s_ring,
    s_leaf,
    s_sib,
    s_w,
    s_wsib,
    s_att,
    s_x,
    s_f,
    r_ring,
    r_leaf,
    r_sib,
    r_w,
    r_att,
    r_x,
    r_f,
):
    ctx = lax.axis_index("ctx")
    head = lax.axis_index("head")
    x, yh = head % 4, head // 4
    q, z, c = ctx // 16, (ctx // 2) % 8, ctx % 2
    y = yh * 4 + q

    def device(dx, dy, dz, dc):
        return {"ctx": ((dy % 4) * 8 + dz) * 2 + dc, "head": (dy // 4) * 4 + dx}

    z_up = device(x, y, (z + 1) % 8, c)
    z_down = device(x, y, (z + 7) % 8, c)
    sibling = device(x, y, z, 1 - c)
    lead = jnp.where(c == 0, x, q)
    two = jnp.where(q % 2 == 0, 2, 6)

    def leaf(delta):
        step = two if delta == 2 else (delta if delta == 1 else 7)
        return device(
            jnp.where(c == 0, (x + delta) % 4, x), jnp.where(c == 0, y, (y + step) % 8), z, c
        )

    x0 = 2 * (q % 2)
    role = (x - x0 + 4) % 4
    my_j = jnp.where((role == 1) | (role == 2), 1, 0)
    my_pair = role // 2

    def target(b):
        return x0 + my_j, 4 * (q // 2) + 2 * my_pair + b // 2, b % 2

    def is_me(dx, dy, dc):
        return (dx == x) & (dy == y) & (dc == c)

    def copy(src, dst, ssem, rsem, dev):
        return pltpu.make_async_remote_copy(
            src_ref=src, dst_ref=dst, send_sem=ssem, recv_sem=rsem, device_id=dev, device_id_type=MESH
        )

    def w_rows(qp, core):
        return wbuf.at[pl.ds(pl.multiple_of(qp * 256 + core * 128, 128), COLS)]

    loads = [
        pltpu.make_async_copy(src, dst, s_in.at[n])
        for n, (src, dst) in enumerate(
            (
                (span_hbm, span_ref),
                (cache_hbm, cache_ref),
                (query_hbm, query_ref),
                (kv_hbm, kv_ref),
                (w_hbm, w_rows(q, c)),
            )
        )
    ]
    for load in loads:
        load.start()

    barrier = pltpu.get_barrier_semaphore()

    def greet(dev):
        pl.semaphore_signal(barrier, inc=1, device_id=dev, device_id_type=MESH)

    greet(z_up)
    greet(z_down)
    greet(sibling)
    for d in (1, 2, 3):
        greet(device((x + d) % 4, y, z, c))
    for d in (1, 2, 6, 7):
        greet(device(x, (y + d) % 8, z, c))
    src_q = 2 * yh + x // 2
    src_j = x % 2
    src_x = jnp.where(q // 2 == 0, x, (2 * (x // 2) + 3 - src_j) % 4)
    for b in range(4):
        sx, sy, sc = src_x, src_q + 4 * (b // 2), b % 2

        @pl.when(jnp.logical_not(is_me(sx, sy, sc)))
        def _():
            greet(device(sx, sy, z, sc))

    selfs = 0
    for b in range(4):
        selfs = selfs + jnp.where(is_me(*target(b)), 1, 0)

    for n in range(8):
        wbuf[n * 128 + COLS : (n + 1) * 128] = jnp.zeros((128 - COLS, 1024), jnp.bfloat16)
    loads[0].wait()
    loads[1].wait()

    mine[:CROWS, :LATENT] = cache_ref[:, :LATENT]
    mine[CROWS:, :LATENT] = span_ref[:, :LATENT]
    mine[:CROWS, LATENT:] = jnp.concatenate(
        [cache_ref[:, LATENT:], jnp.zeros((CROWS, 64), jnp.bfloat16)], axis=1
    )
    mine[CROWS:, LATENT:] = jnp.concatenate(
        [span_ref[:, LATENT:], jnp.zeros((TOK, 64), jnp.bfloat16)], axis=1
    )

    def slot(zp, qp):
        return keys.at[zp, pl.ds(pl.multiple_of(c * HALF + qp * SHARD, SHARD), SHARD)]

    has_primary = (c == 1) | (q == x)

    @pl.when(has_primary)
    def _():
        slot(z, lead)[...] = mine[...]

    pl.semaphore_wait(barrier, 2 + 1 + 3 + 4 + 4 - selfs)

    def at(k):
        return (z + 8 + jnp.where(k % 2 == 1, -((k + 1) // 2), k // 2)) % 8

    def pre(n):
        d = (1, 2, 7)[n]
        return copy(mine, slot(z, x), s_pre.at[n], r_ring.at[z * 4 + x], device(x, (y + d) % 8, z, c))

    sends_pre = (c == 0) & (q == x)

    @pl.when(sends_pre)
    def _():
        for n in range(3):
            pre(n).start()

    @pl.when(jnp.logical_not(has_primary))
    def _():
        pre(0).wait_recv()

    def ring_copy(k, qp, sem, dev):
        piece = slot(at(k), qp)
        return copy(piece, piece, s_ring.at[sem], r_ring.at[at(k) * 4 + qp], dev)

    def leaf_copy(k, n):
        piece = slot(at(k), lead)
        d = (1, 3, 2)[n]
        return copy(piece, piece, s_leaf.at[3 * k + n], r_leaf.at[at(k) * 4 + lead], leaf(d))

    def leaf_wait(k, d):
        qp = (lead + d) % 4
        piece = slot(at(k), qp)
        copy(piece, piece, s_leaf.at[0], r_leaf.at[at(k) * 4 + qp], leaf(1)).wait_recv()
        return qp

    def forward(k, qp, low, high):
        ring_copy(k, qp, 0, z_up).wait_recv()

        @pl.when((k % 2 == 1) & ((k < 5) | (low & (k == 5))))
        def _():
            ring_copy(k, qp, 4 * k + qp, z_up).start()

        @pl.when((k % 2 == 0) & ((k < 6) | (high & (k == 6))))
        def _():
            ring_copy(k, qp, 4 * k + qp, z_down).start()

    def first(qp):
        ring_copy(0, qp, qp, z_up).start()
        ring_copy(0, qp, 28 + qp, z_down).start()

    def stage1(k):
        @pl.when(c == 0)
        def _():
            forward(k, lead, True, False)
            for n in range(3):
                leaf_copy(k, n).start()

        @pl.when(c == 1)
        def _():
            for qp in range(4):
                forward(k, qp, qp < 2, qp >= 2)
            sib_copy(k).start()

    def half(zp, core):
        return keys.at[zp, pl.ds(pl.multiple_of(core * HALF, HALF), HALF)]

    def sib_copy(k):
        zp = at(k)
        return copy(half(zp, c), half(zp, c), s_sib.at[k], r_sib.at[zp], sibling)

    def stage2(k):
        @pl.when(c == 0)
        def _():
            for d in (1, 3, 2):
                leaf_wait(k, d)
            sib_copy(k).start()

    place = lax.broadcasted_iota(jnp.int32, (1, BLOCK), 1)
    core_of = jnp.where(place >= HALF, 1, 0)
    within = place - core_of * HALF
    plane = sum(jnp.where(within >= n * SHARD, 1, 0) for n in (1, 2, 3))
    row = within - plane * SHARD
    token_base = plane * 1024 + core_of * TOK + row - CROWS
    cache_base = plane * 256 + core_of * CROWS + row
    cached = row < CROWS
    length = length_ref[0]

    def flash(zs, start, count):
        rows = pl.ds(start, count)
        token = ctx * TOK + lax.broadcasted_iota(jnp.int32, (count, 1), 0) % TOK
        scores = []
        for zp in zs:
            code = jnp.where(
                cached,
                jnp.where(cache_base + zp * 32 < length, -1, FAR),
                token_base + zp * 128,
            )
            product = lax.dot_general(
                queries[rows], keys[zp], (((1,), (1,)), ((), ())), preferred_element_type=jnp.float32
            )
            scores.append(jnp.where(code <= token, product * SCALE2, MASKED))
        before = maxima[rows, :1]
        raised = before
        for part_scores in scores:
            raised = jnp.maximum(raised, jnp.max(part_scores, axis=1, keepdims=True))
        factor = jnp.exp2(before - raised)
        maxima[rows] = jnp.broadcast_to(raised, (count, 128))
        total = totals[rows] * factor
        value = acc[rows] * factor
        for zp, part_scores in zip(zs, scores):
            weights = jnp.exp2(part_scores - raised)
            total = total + jnp.sum(weights, axis=1, keepdims=True)
            value = value + jnp.dot(
                weights.astype(jnp.bfloat16), keys[zp, :, :LATENT], preferred_element_type=jnp.float32
            )
        totals[rows] = total
        acc[rows] = value

    first(lead)
    for n in range(3):
        leaf_copy(0, n).start()

    def w_move(qp, sem, dev):
        return copy(w_rows(qp, c), w_rows(qp, c), s_w.at[sem], r_w.at[qp * 2 + c], dev)

    def w_sib(qp):
        return copy(w_rows(qp, c), w_rows(qp, c), s_wsib.at[qp], r_w.at[qp * 2 + c], sibling)

    def w_wait(qp, core):
        copy(w_rows(qp, core), w_rows(qp, core), s_w.at[0], r_w.at[qp * 2 + core], sibling).wait_recv()

    y_up = device(x, (y + 1) % 8, z, c)
    y_down = device(x, (y + 7) % 8, z, c)

    def w_round(n):
        @pl.when(q >= n)
        def _():
            if n > 0:
                w_wait(q - n, c)
                w_sib(q - n).start()

            @pl.when(q < 3)
            def _():
                w_move(q - n, n, y_up).start()

        @pl.when(q + n < 4)
        def _():
            if n > 0:
                w_wait(q + n, c)
                w_sib(q + n).start()

            @pl.when(q > 0)
            def _():
                w_move(q + n, 3 + n, y_down).start()

    loads[4].wait()
    w_round(0)
    w_sib(q).start()
    loads[2].wait()
    loads[3].wait()

    for h in range(HEADS):
        nope = query_ref[:, h * 192 : h * 192 + NOPE]
        rope = query_ref[:, h * 192 + NOPE : (h + 1) * 192]
        absorbed = lax.dot_general(
            nope,
            kv_ref[:, h * 256 : h * 256 + NOPE],
            (((1,), (1,)), ((), ())),
            preferred_element_type=jnp.float32,
        ).astype(jnp.bfloat16)
        queries[h * TOK : (h + 1) * TOK, :LATENT] = absorbed
        queries[h * TOK : (h + 1) * TOK, LATENT:] = jnp.concatenate(
            [rope, jnp.zeros((TOK, 64), jnp.bfloat16)], axis=1
        )
    maxima[...] = jnp.full((ROWS, 128), MASKED, jnp.float32)
    totals[...] = jnp.zeros((ROWS, 128), jnp.float32)
    acc[...] = jnp.zeros((ROWS, LATENT), jnp.float32)

    @pl.when(c == 1)
    def _():
        for d in (1, 3, 2):
            first(leaf_wait(0, d))
        sib_copy(0).start()

    def body(j, carry):
        for n in (0, 1):
            k = 2 * j + 1 + n

            @pl.when(k < 8)
            def _():
                stage1(k)

        @pl.when(j == 1)
        def _():
            sib_copy(0).wait_recv()
            flash([z], 0, ROWS)

        @pl.when(j > 1)
        def _():
            ks = (2 * j - 3, 2 * j - 2)
            for k in ks:
                sib_copy(k).wait_recv()
            flash([at(k) for k in ks], 0, ROWS)

        for n in (0, 1):
            k = 2 * j - 1 + n

            @pl.when((k >= 0) & (k < 8))
            def _():
                stage2(k)

        @pl.when(j == 2)
        def _():
            w_round(1)

        @pl.when(j == 3)
        def _():
            w_round(2)

        return carry

    lax.fori_loop(0, 5, body, 0)

    def att_copy(k, hf, sem, dev):
        piece = att.at[at(k), :, pl.ds(hf * 512, 512)]
        return copy(piece, piece, s_att.at[sem], r_att.at[at(k) * 2 + hf], dev)

    sib_copy(7).wait_recv()
    for hf in (0, 1):
        rows = pl.ds(hf * 256, 256)
        flash([at(7)], hf * 256, 256)
        latent_out[rows] = (acc[rows] / totals[rows, :1]).astype(jnp.bfloat16)
        for h in range(4 * hf, 4 * hf + 4):
            att[z, :, h * VDIM : (h + 1) * VDIM] = jnp.dot(
                latent_out[h * TOK : (h + 1) * TOK],
                kv_ref[:, h * 256 + NOPE : (h + 1) * 256],
                preferred_element_type=jnp.float32,
            ).astype(jnp.bfloat16)
        att_copy(0, hf, hf, z_up).start()
        att_copy(0, hf, 14 + hf, z_down).start()

    @pl.when(q == 3)
    def _():
        w_wait(0, c)
        w_sib(0).start()

    @pl.when(q == 0)
    def _():
        w_wait(3, c)
        w_sib(3).start()

    for qp in range(4):
        w_wait(qp, 1 - c)

    def collector(zp, pair):
        j = zp // 4
        return (x0 + jnp.where(pair == 0, j, 3 - j)) % 4

    def x_copy(zp, pair):
        r = collector(zp, pair)
        return r, copy(
            part.at[zp, :, pl.ds(pair * 512, 512)],
            landed.at[x, zp % 4],
            s_x.at[zp * 2 + pair],
            r_x.at[x * 4 + zp % 4],
            device(r, y, z, c),
        )

    def project(zs):
        rows = jnp.concatenate([att[zp] for zp in zs], axis=0)
        product = lax.dot_general(
            rows, wbuf[...], (((1,), (1,)), ((), ())), preferred_element_type=jnp.float32
        ).astype(jnp.bfloat16)
        for n, zp in enumerate(zs):
            part[zp] = product[n * TOK : (n + 1) * TOK]
            for pair in (0, 1):
                r, cp = x_copy(zp, pair)

                @pl.when(r != x)
                def _():
                    cp.start()

    me_slot = yh * 2 + c

    def final_parts(b, zi):
        rows = pl.ds(pl.multiple_of(zi * TOK, TOK), TOK)
        return reduced.at[rows, pl.ds(b * 128, 128)], final.at[me_slot, rows]

    def final_copy(b, zi):
        dx, dy, dc = target(b)
        src, dst = final_parts(b, zi)
        return copy(src, dst, s_f.at[b * 4 + zi], r_f.at[me_slot * 4 + zi], device(dx, dy, z, dc))

    def reduce(k):
        zp = at(k)
        zi = zp % 4

        @pl.when(zp // 4 == my_j)
        def _():
            lanes = pl.ds(pl.multiple_of(my_pair * 512, 512), 512)
            total = part[zp, :, lanes].astype(jnp.float32)
            for d in (1, 2, 3):
                xs = (x + d) % 4
                copy(landed.at[xs, zi], landed.at[xs, zi], s_x.at[0], r_x.at[xs * 4 + zi], sibling).wait_recv()
                total = total + landed[xs, zi].astype(jnp.float32)
            reduced[pl.ds(pl.multiple_of(zi * TOK, TOK), TOK)] = total.astype(jnp.bfloat16)
            for b in range(4):
                here = is_me(*target(b))

                @pl.when(here)
                def _():
                    src, dst = final_parts(b, zi)
                    pltpu.make_async_copy(src, dst, r_f.at[me_slot * 4 + zi]).start()

                @pl.when(jnp.logical_not(here))
                def _():
                    final_copy(b, zi).start()

    project([z])

    def out_step(j, carry):
        ks = (2 * j - 1, 2 * j)
        for k in ks:

            @pl.when(k < 8)
            def _():
                for hf in (0, 1):
                    att_copy(k, hf, 0, z_up).wait_recv()

                    @pl.when((k % 2 == 1) & ((k < 5) | ((k == 5) & (hf == 0))))
                    def _():
                        att_copy(k, hf, 2 * k + hf, z_up).start()

                    @pl.when((k % 2 == 0) & ((k < 6) | ((k == 6) & (hf == 1))))
                    def _():
                        att_copy(k, hf, 2 * k + hf, z_down).start()

        @pl.when(j < 4)
        def _():
            project([at(k) for k in ks])

        @pl.when(j == 4)
        def _():
            project([at(7)])

        reduce(2 * j - 2)

        @pl.when(j > 1)
        def _():
            reduce(2 * j - 3)

        return carry

    lax.fori_loop(1, 5, out_step, 0)
    reduce(7)

    for core in range(2):
        for h in range(2):
            n = h * 2 + core
            for zi in range(4):
                dst = final.at[n, pl.ds(zi * TOK, TOK)]
                copy(dst, dst, s_f.at[0], r_f.at[n * 4 + zi], sibling).wait_recv()
        total = final[core].astype(jnp.float32) + final[2 + core].astype(jnp.float32)
        total = total[:, :COLS].astype(jnp.bfloat16)
        for zi in range(4):
            out_ref[zi * 128 + core * TOK : zi * 128 + (core + 1) * TOK] = total[zi * TOK : (zi + 1) * TOK]

    @pl.when(sends_pre)
    def _():
        for n in range(3):
            pre(n).wait_send()

    @pl.when(c == 0)
    def _():
        for k in range(6):
            ring_copy(0, lead, 4 * k + lead, z_up).wait_send()
        ring_copy(0, lead, 28 + lead, z_up).wait_send()
        for k in range(8):
            for n in range(3):
                leaf_copy(k, n).wait_send()

    @pl.when(c == 1)
    def _():
        for n in range(24):
            if n not in (22, 23):
                ring_copy(0, 0, n, z_up).wait_send()
        for n in (26, 27, 28, 29, 30, 31):
            ring_copy(0, 0, n, z_up).wait_send()
        for n in range(3):
            leaf_copy(0, n).wait_send()

    for k in range(8):
        sib_copy(k).wait_send()
    for n in range(3):

        @pl.when((q >= n) & (q < 3))
        def _():
            w_move(0, n, y_up).wait_send()

        @pl.when((q + n < 4) & (q > 0))
        def _():
            w_move(0, 3 + n, y_down).wait_send()

    for qp in range(4):
        w_sib(qp).wait_send()
    for n in range(16):
        if n not in (11, 12):
            att_copy(0, 0, n, z_up).wait_send()
    for zp in range(8):
        for pair in (0, 1):
            r, cp = x_copy(zp, pair)

            @pl.when(r != x)
            def _():
                cp.wait_send()

    for b in range(4):

        @pl.when(jnp.logical_not(is_me(*target(b))))
        def _():
            for zi in range(4):
                final_copy(b, zi).wait_send()


def on_device(span_query, span_latent, cache_latent, cache_length, kv_up_weight, out_weight):
    vmem = pl.BlockSpec(memory_space=pltpu.VMEM)
    hbm = pl.BlockSpec(memory_space=pltpu.HBM)
    dma = pltpu.SemaphoreType.DMA
    return pl.pallas_call(
        kernel,
        out_shape=jax.ShapeDtypeStruct((512, COLS), jnp.bfloat16),
        in_specs=[hbm, hbm, hbm, pl.BlockSpec(memory_space=pltpu.SMEM), hbm, hbm],
        out_specs=vmem,
        scratch_shapes=[
            pltpu.VMEM((TOK, HEADS * 192), jnp.bfloat16),
            pltpu.VMEM((TOK, LATENT + ROPE), jnp.bfloat16),
            pltpu.VMEM((CROWS, LATENT + ROPE), jnp.bfloat16),
            pltpu.VMEM((LATENT, HEADS * 256), jnp.bfloat16),
            pltpu.VMEM((8, BLOCK, WIDE), jnp.bfloat16),
            pltpu.VMEM((SHARD, WIDE), jnp.bfloat16),
            pltpu.VMEM((ROWS, WIDE), jnp.bfloat16),
            pltpu.VMEM((ROWS, 128), jnp.float32),
            pltpu.VMEM((ROWS, 128), jnp.float32),
            pltpu.VMEM((ROWS, LATENT), jnp.float32),
            pltpu.VMEM((ROWS, LATENT), jnp.bfloat16),
            pltpu.VMEM((1024, 1024), jnp.bfloat16),
            pltpu.VMEM((8, TOK, 1024), jnp.bfloat16),
            pltpu.VMEM((8, TOK, 1024), jnp.bfloat16),
            pltpu.VMEM((4, 4, TOK, 512), jnp.bfloat16),
            pltpu.VMEM((4 * TOK, 512), jnp.bfloat16),
            pltpu.VMEM((4, 4 * TOK, 128), jnp.bfloat16),
            dma((5,)),
            dma((3,)),
            dma((32,)),
            dma((24,)),
            dma((8,)),
            dma((6,)),
            dma((4,)),
            dma((16,)),
            dma((16,)),
            dma((16,)),
            dma((32,)),
            dma((32,)),
            dma((8,)),
            dma((8,)),
            dma((16,)),
            dma((16,)),
            dma((16,)),
        ],
        compiler_params=pltpu.CompilerParams(
            collective_id=0, has_side_effects=True, vmem_limit_bytes=63 << 20
        ),
        cost_estimate=pl.CostEstimate(
            flops=8_000_000_000, bytes_accessed=4_000_000, transcendentals=2_600_000
        ),
        name="mla_prefill",
    )(span_query, span_latent, cache_latent, cache_length, kv_up_weight, out_weight.T)


def solution(mesh):
    return jax.shard_map(
        on_device,
        mesh=mesh,
        in_specs=(
            P("ctx", "head"),
            P("ctx", None),
            P("ctx", None),
            P(),
            P(None, "head"),
            P("head", "ctx"),
        ),
        out_specs=P("head", "ctx"),
        check_vma=False,
    )
```

```python
import math

import jax
import jax.numpy as jnp
from jax import lax
from jax.experimental import pallas as pl
from jax.experimental.pallas import tpu as pltpu
from jax.sharding import PartitionSpec as P

LATENT = 512
ROPE = 64
NOPE = 128
VDIM = 128
HEADS = 8
TOK = 64
CROWS = 16
SHARD = TOK + CROWS
WIDE = 640
HALF = 4 * SHARD
BLOCK = 2 * HALF
COLS = 112
ROWS = HEADS * TOK
MASKED = -1e30
FAR = 1 << 30
MESH = pl.DeviceIdType.MESH
SCALE2 = (1.0 + 0.1 * math.log(40.0)) ** 2 / math.sqrt(NOPE + ROPE) * math.log2(math.e)


def kernel(
    query_hbm,
    span_hbm,
    cache_hbm,
    length_ref,
    kv_hbm,
    w_hbm,
    out_ref,
    query_ref,
    span_ref,
    cache_ref,
    kv_ref,
    keys,
    mine,
    queries,
    maxima,
    totals,
    acc,
    latent_out,
    wbuf,
    att,
    part,
    landed,
    reduced,
    final,
    s_in,
    s_pre,
    s_ring,
    s_leaf,
    s_far,
    s_sib,
    s_w,
    s_wsib,
    s_att,
    s_x,
    s_f,
    r_ring,
    r_leaf,
    r_far,
    r_sib,
    r_w,
    r_att,
    r_x,
    r_f,
):
    ctx = lax.axis_index("ctx")
    head = lax.axis_index("head")
    x, yh = (head & 3), (head >> 2)
    q, z, c = (ctx >> 4), (((ctx >> 1)) & 7), (ctx & 1)
    y = yh * 4 + q

    def device(dx, dy, dz, dc):
        return {"ctx": (((dy & 3)) * 8 + dz) * 2 + dc, "head": ((dy >> 2)) * 4 + dx}

    z_up = device(x, y, ((z + 1) & 7), c)
    z_down = device(x, y, ((z + 7) & 7), c)
    sibling = device(x, y, z, 1 - c)
    lead = jnp.where(c == 0, x, q)

    def leaf(delta):
        step = 1 if delta == 1 else 7
        return device(
            jnp.where(c == 0, ((x + delta) & 3), x), jnp.where(c == 0, y, ((y + step) & 7)), z, c
        )

    x0 = 2 * ((q & 1))
    role = ((x - x0 + 4) & 3)
    my_j = jnp.where((role == 1) | (role == 2), 1, 0)
    my_pair = (role >> 1)

    def target(b):
        return x0 + my_j, 4 * ((q >> 1)) + 2 * my_pair + (b >> 1), (b & 1)

    def is_me(dx, dy, dc):
        return (dx == x) & (dy == y) & (dc == c)

    def copy(src, dst, ssem, rsem, dev):
        return pltpu.make_async_remote_copy(
            src_ref=src, dst_ref=dst, send_sem=ssem, recv_sem=rsem, device_id=dev, device_id_type=MESH
        )

    def w_rows(qp, core):
        return wbuf.at[pl.ds(pl.multiple_of(qp * 256 + core * 128, 128), COLS)]

    loads = [
        pltpu.make_async_copy(src, dst, s_in.at[n])
        for n, (src, dst) in enumerate(
            (
                (span_hbm, span_ref),
                (cache_hbm, cache_ref),
                (query_hbm, query_ref),
                (kv_hbm, kv_ref),
                (w_hbm, w_rows(q, c)),
            )
        )
    ]
    for load in loads:
        load.start()

    barrier = pltpu.get_barrier_semaphore()

    def greet(dev):
        pl.semaphore_signal(barrier, inc=1, device_id=dev, device_id_type=MESH)

    for dev in (z_up, z_down):
        greet(dev)
    greet(sibling)
    for d in (1, 2, 3):
        greet(device(((x + d) & 3), y, z, c))
    for d in (1, 2, 6, 7):
        greet(device(x, ((y + d) & 7), z, c))
    src_q = 2 * yh + (x >> 1)
    src_j = (x & 1)
    src_x = jnp.where((q >> 1) == 0, x, ((2 * ((x >> 1)) + 3 - src_j) & 3))
    for b in range(4):
        sx, sy, sc = src_x, src_q + 4 * ((b >> 1)), (b & 1)

        @pl.when(jnp.logical_not(is_me(sx, sy, sc)))
        def _():
            greet(device(sx, sy, z, sc))

    selfs = 0
    for b in range(4):
        selfs = selfs + jnp.where(is_me(*target(b)), 1, 0)

    for n in range(8):
        wbuf[n * 128 + COLS : (n + 1) * 128] = jnp.zeros((128 - COLS, 1024), jnp.bfloat16)
    loads[0].wait()
    loads[1].wait()

    mine[:CROWS, :LATENT] = cache_ref[:, :LATENT]
    mine[CROWS:, :LATENT] = span_ref[:, :LATENT]
    mine[:CROWS, LATENT:] = jnp.concatenate(
        [cache_ref[:, LATENT:], jnp.zeros((CROWS, 64), jnp.bfloat16)], axis=1
    )
    mine[CROWS:, LATENT:] = jnp.concatenate(
        [span_ref[:, LATENT:], jnp.zeros((TOK, 64), jnp.bfloat16)], axis=1
    )

    def slot(zp, qp):
        return keys.at[zp, pl.ds(pl.multiple_of(c * HALF + qp * SHARD, SHARD), SHARD)]

    has_primary = (c == 1) | (q == x)

    @pl.when(has_primary)
    def _():
        slot(z, lead)[...] = mine[...]

    pl.semaphore_wait(barrier, 2 + 1 + 3 + 4 + 4 - selfs)

    def at(k):
        return (z + 8 + jnp.where((k & 1) == 1, -(((k + 1) >> 1)), (k >> 1))) % 8

    def pre(n):
        d = (1, 2, 7)[n]
        return copy(mine, slot(z, x), s_pre.at[n], r_ring.at[z * 4 + x], device(x, ((y + d) & 7), z, c))

    sends_pre = (c == 0) & (q == x)

    @pl.when(sends_pre)
    def _():
        for n in range(3):
            pre(n).start()

    @pl.when(jnp.logical_not(has_primary))
    def _():
        pre(0).wait_recv()

    def ring_copy(k, qp, sem, dev):
        piece = slot(at(k), qp)
        return copy(piece, piece, s_ring.at[sem], r_ring.at[at(k) * 4 + qp], dev)

    def leaf_copy(k, n):
        piece = slot(at(k), lead)
        d = (1, 3)[n]
        return copy(piece, piece, s_leaf.at[3 * k + n], r_leaf.at[at(k) * 4 + lead], leaf(d))

    def leaf_wait(k, d):
        qp = ((lead + d) & 3)
        piece = slot(at(k), qp)
        copy(piece, piece, s_leaf.at[0], r_leaf.at[at(k) * 4 + qp], leaf(1)).wait_recv()
        return qp

    def forward(k, qp, low, high):
        ring_copy(k, qp, 0, z_up).wait_recv()

        @pl.when(((k & 1) == 1) & ((k < 5) | (low & (k == 5))))
        def _():
            ring_copy(k, qp, 4 * k + qp, z_up).start()

        @pl.when(((k & 1) == 0) & ((k < 6) | (high & (k == 6))))
        def _():
            ring_copy(k, qp, 4 * k + qp, z_down).start()

    def first(qp):
        ring_copy(0, qp, qp, z_up).start()
        ring_copy(0, qp, 28 + qp, z_down).start()

    def stage1(k):
        forward(k, lead, True, False)
        for n in range(2):
            leaf_copy(k, n).start()

    def half(zp, core):
        return keys.at[zp, pl.ds(pl.multiple_of(core * HALF, HALF), HALF)]

    def sib_copy(k):
        zp = at(k)
        return copy(half(zp, c), half(zp, c), s_sib.at[k], r_sib.at[zp], sibling)

    def pass_copy(k, n, qp):
        start, rows = ((0, 48), (48, 32))[n]
        first_row = pl.multiple_of(c * HALF + qp * SHARD, SHARD) + start
        piece = keys.at[at(k), pl.ds(first_row, rows)]
        sem = (r_leaf.at[at(k) * 4 + qp], r_far.at[at(k)])[n]
        return copy(piece, piece, s_far.at[2 * k + n], sem, leaf((3, 1)[n]))

    def stage2(k):
        for n, d in enumerate((1, 3)):
            qp = leaf_wait(k, d)
            pass_copy(k, n, qp).start()

    def stage3(k):
        for n in range(2):
            pass_copy(k, n, (lead + 2) & 3).wait_recv()
        sib_copy(k).start()

    place = lax.broadcasted_iota(jnp.int32, (1, BLOCK), 1)
    core_of = jnp.where(place >= HALF, 1, 0)
    within = place - core_of * HALF
    plane = sum(jnp.where(within >= n * SHARD, 1, 0) for n in (1, 2, 3))
    row = within - plane * SHARD
    token_base = plane * 1024 + core_of * TOK + row - CROWS
    cache_base = plane * 256 + core_of * CROWS + row
    cached = row < CROWS
    length = length_ref[0]

    def flash(zs, start, count):
        rows = pl.ds(start, count)
        token = ctx * TOK + (lax.broadcasted_iota(jnp.int32, (count, 1), 0) & (TOK - 1))
        scores = []
        for zp in zs:
            code = jnp.where(
                cached,
                jnp.where(cache_base + zp * 32 < length, -1, FAR),
                token_base + zp * 128,
            )
            product = lax.dot_general(
                queries[rows], keys[zp], (((1,), (1,)), ((), ())), preferred_element_type=jnp.float32
            )
            scores.append(jnp.where(code <= token, product * SCALE2, MASKED))
        before = maxima[rows, :1]
        raised = before
        for part_scores in scores:
            raised = jnp.maximum(raised, jnp.max(part_scores, axis=1, keepdims=True))
        factor = jnp.exp2(before - raised)
        maxima[rows] = jnp.broadcast_to(raised, (count, 128))
        total = totals[rows] * factor
        value = acc[rows] * factor
        for zp, part_scores in zip(zs, scores):
            weights = jnp.exp2(part_scores - raised)
            total = total + jnp.sum(weights, axis=1, keepdims=True)
            value = value + jnp.dot(
                weights.astype(jnp.bfloat16), keys[zp, :, :LATENT], preferred_element_type=jnp.float32
            )
        totals[rows] = total
        acc[rows] = value

    first(lead)
    for n in range(2):
        leaf_copy(0, n).start()

    def w_move(qp, sem, dev):
        return copy(w_rows(qp, c), w_rows(qp, c), s_w.at[sem], r_w.at[qp * 2 + c], dev)

    def w_sib(qp):
        return copy(w_rows(qp, c), w_rows(qp, c), s_wsib.at[qp], r_w.at[qp * 2 + c], sibling)

    def w_wait(qp, core):
        copy(w_rows(qp, core), w_rows(qp, core), s_w.at[0], r_w.at[qp * 2 + core], sibling).wait_recv()

    y_up = device(x, ((y + 1) & 7), z, c)
    y_down = device(x, ((y + 7) & 7), z, c)

    def w_round(n):
        @pl.when(q >= n)
        def _():
            if n > 0:
                w_wait(q - n, c)
                w_sib(q - n).start()

            @pl.when(q < 3)
            def _():
                w_move(q - n, n, y_up).start()

        @pl.when(q + n < 4)
        def _():
            if n > 0:
                w_wait(q + n, c)
                w_sib(q + n).start()

            @pl.when(q > 0)
            def _():
                w_move(q + n, 3 + n, y_down).start()

    loads[4].wait()
    w_round(0)
    w_sib(q).start()
    loads[2].wait()
    loads[3].wait()

    for h in range(HEADS):
        nope = query_ref[:, h * 192 : h * 192 + NOPE]
        rope = query_ref[:, h * 192 + NOPE : (h + 1) * 192]
        absorbed = lax.dot_general(
            nope,
            kv_ref[:, h * 256 : h * 256 + NOPE],
            (((1,), (1,)), ((), ())),
            preferred_element_type=jnp.float32,
        ).astype(jnp.bfloat16)
        queries[h * TOK : (h + 1) * TOK, :LATENT] = absorbed
        queries[h * TOK : (h + 1) * TOK, LATENT:] = jnp.concatenate(
            [rope, jnp.zeros((TOK, 64), jnp.bfloat16)], axis=1
        )
    maxima[...] = jnp.full((ROWS, 128), MASKED, jnp.float32)
    totals[...] = jnp.zeros((ROWS, 128), jnp.float32)
    acc[...] = jnp.zeros((ROWS, LATENT), jnp.float32)

    def pair_of(g, stage):
        for k in (2 * g - 1, 2 * g):

            @pl.when((k >= 0) & (k < 8))
            def _():
                stage(k)

    def attend(g):
        @pl.when(g == 0)
        def _():
            sib_copy(0).wait_recv()
            flash([z], 0, ROWS)

        @pl.when(g > 0)
        def _():
            ks = (2 * g - 1, 2 * g)
            for k in ks:
                sib_copy(k).wait_recv()
            flash([at(k) for k in ks], 0, ROWS)

    def w_last():
        @pl.when(q == 3)
        def _():
            w_wait(0, c)
            w_sib(0).start()

        @pl.when(q == 0)
        def _():
            w_wait(3, c)
            w_sib(3).start()

    def body(j, carry):
        @pl.when(j < 4)
        def _():
            pair_of(j + 1, stage1)

        @pl.when(j < 5)
        def _():
            pair_of(j, stage2)

        @pl.when(j > 0)
        def _():
            pair_of(j - 1, stage3)

        @pl.when(j == 1)
        def _():
            w_round(1)

        @pl.when(j == 3)
        def _():
            w_round(2)

        @pl.when(j == 5)
        def _():
            w_last()

        @pl.when(j > 1)
        def _():
            attend(j - 2)

        return carry

    lax.fori_loop(0, 6, body, 0)

    def att_copy(k, hf, sem, dev):
        piece = att.at[at(k), :, pl.ds(hf * 512, 512)]
        return copy(piece, piece, s_att.at[sem], r_att.at[at(k) * 2 + hf], dev)

    sib_copy(7).wait_recv()
    for hf in (0, 1):
        rows = pl.ds(hf * 256, 256)
        flash([at(7)], hf * 256, 256)
        latent_out[rows] = (acc[rows] / totals[rows, :1]).astype(jnp.bfloat16)
        for h in range(4 * hf, 4 * hf + 4):
            att[z, :, h * VDIM : (h + 1) * VDIM] = jnp.dot(
                latent_out[h * TOK : (h + 1) * TOK],
                kv_ref[:, h * 256 + NOPE : (h + 1) * 256],
                preferred_element_type=jnp.float32,
            ).astype(jnp.bfloat16)
        att_copy(0, hf, hf, z_up).start()
        att_copy(0, hf, 14 + hf, z_down).start()

    for qp in range(4):
        w_wait(qp, 1 - c)

    def collector(zp, pair):
        j = (zp >> 2)
        return ((x0 + jnp.where(pair == 0, j, 3 - j)) & 3)

    def x_copy(zp, pair):
        r = collector(zp, pair)
        return r, copy(
            part.at[zp, :, pl.ds(pair * 512, 512)],
            landed.at[x, (zp & 3)],
            s_x.at[zp * 2 + pair],
            r_x.at[x * 4 + (zp & 3)],
            device(r, y, z, c),
        )

    def project(zs):
        rows = jnp.concatenate([att[zp] for zp in zs], axis=0)
        product = lax.dot_general(
            rows, wbuf[...], (((1,), (1,)), ((), ())), preferred_element_type=jnp.float32
        ).astype(jnp.bfloat16)
        for n, zp in enumerate(zs):
            part[zp] = product[n * TOK : (n + 1) * TOK]
            for pair in (0, 1):
                r, cp = x_copy(zp, pair)

                @pl.when(r != x)
                def _():
                    cp.start()

    me_slot = yh * 2 + c

    def final_parts(b, zi):
        rows = pl.ds(pl.multiple_of(zi * TOK, TOK), TOK)
        return reduced.at[rows, pl.ds(b * 128, 128)], final.at[me_slot, rows]

    def final_copy(b, zi):
        dx, dy, dc = target(b)
        src, dst = final_parts(b, zi)
        return copy(src, dst, s_f.at[b * 4 + zi], r_f.at[me_slot * 4 + zi], device(dx, dy, z, dc))

    def reduce(k):
        zp = at(k)
        zi = (zp & 3)

        @pl.when((zp >> 2) == my_j)
        def _():
            lanes = pl.ds(pl.multiple_of(my_pair * 512, 512), 512)
            total = part[zp, :, lanes].astype(jnp.float32)
            for d in (1, 2, 3):
                xs = ((x + d) & 3)
                copy(landed.at[xs, zi], landed.at[xs, zi], s_x.at[0], r_x.at[xs * 4 + zi], sibling).wait_recv()
                total = total + landed[xs, zi].astype(jnp.float32)
            reduced[pl.ds(pl.multiple_of(zi * TOK, TOK), TOK)] = total.astype(jnp.bfloat16)
            for b in range(4):
                here = is_me(*target(b))

                @pl.when(here)
                def _():
                    src, dst = final_parts(b, zi)
                    pltpu.make_async_copy(src, dst, r_f.at[me_slot * 4 + zi]).start()

                @pl.when(jnp.logical_not(here))
                def _():
                    final_copy(b, zi).start()

    project([z])

    def out_step(j, carry):
        ks = (2 * j - 1, 2 * j)
        for k in ks:

            @pl.when(k < 8)
            def _():
                for hf in (0, 1):
                    att_copy(k, hf, 0, z_up).wait_recv()

                    @pl.when(((k & 1) == 1) & ((k < 5) | ((k == 5) & (hf == 0))))
                    def _():
                        att_copy(k, hf, 2 * k + hf, z_up).start()

                    @pl.when(((k & 1) == 0) & ((k < 6) | ((k == 6) & (hf == 1))))
                    def _():
                        att_copy(k, hf, 2 * k + hf, z_down).start()

        @pl.when(j < 4)
        def _():
            project([at(k) for k in ks])

        @pl.when(j == 4)
        def _():
            project([at(7)])

        reduce(2 * j - 2)

        @pl.when(j > 1)
        def _():
            reduce(2 * j - 3)

        return carry

    lax.fori_loop(1, 5, out_step, 0)
    reduce(7)

    for core in range(2):
        for h in range(2):
            n = h * 2 + core
            for zi in range(4):
                dst = final.at[n, pl.ds(zi * TOK, TOK)]
                copy(dst, dst, s_f.at[0], r_f.at[n * 4 + zi], sibling).wait_recv()
        total = final[core].astype(jnp.float32) + final[2 + core].astype(jnp.float32)
        total = total[:, :COLS].astype(jnp.bfloat16)
        for zi in range(4):
            out_ref[zi * 128 + core * TOK : zi * 128 + (core + 1) * TOK] = total[zi * TOK : (zi + 1) * TOK]

    @pl.when(sends_pre)
    def _():
        for n in range(3):
            pre(n).wait_send()

    for k in range(6):
        ring_copy(0, lead, 4 * k + lead, z_up).wait_send()
    ring_copy(0, lead, 28 + lead, z_up).wait_send()
    for k in range(8):
        for n in range(2):
            leaf_copy(k, n).wait_send()
            pass_copy(k, n, lead).wait_send()
    for k in range(8):
        sib_copy(k).wait_send()
    for n in range(3):

        @pl.when((q >= n) & (q < 3))
        def _():
            w_move(0, n, y_up).wait_send()

        @pl.when((q + n < 4) & (q > 0))
        def _():
            w_move(0, 3 + n, y_down).wait_send()

    for qp in range(4):
        w_sib(qp).wait_send()
    for n in range(16):
        if n not in (11, 12):
            att_copy(0, 0, n, z_up).wait_send()
    for zp in range(8):
        for pair in (0, 1):
            r, cp = x_copy(zp, pair)

            @pl.when(r != x)
            def _():
                cp.wait_send()

    for b in range(4):

        @pl.when(jnp.logical_not(is_me(*target(b))))
        def _():
            for zi in range(4):
                final_copy(b, zi).wait_send()


def on_device(span_query, span_latent, cache_latent, cache_length, kv_up_weight, out_weight):
    vmem = pl.BlockSpec(memory_space=pltpu.VMEM)
    hbm = pl.BlockSpec(memory_space=pltpu.HBM)
    dma = pltpu.SemaphoreType.DMA
    return pl.pallas_call(
        kernel,
        out_shape=jax.ShapeDtypeStruct((512, COLS), jnp.bfloat16),
        in_specs=[hbm, hbm, hbm, pl.BlockSpec(memory_space=pltpu.SMEM), hbm, hbm],
        out_specs=vmem,
        scratch_shapes=[
            pltpu.VMEM((TOK, HEADS * 192), jnp.bfloat16),
            pltpu.VMEM((TOK, LATENT + ROPE), jnp.bfloat16),
            pltpu.VMEM((CROWS, LATENT + ROPE), jnp.bfloat16),
            pltpu.VMEM((LATENT, HEADS * 256), jnp.bfloat16),
            pltpu.VMEM((8, BLOCK, WIDE), jnp.bfloat16),
            pltpu.VMEM((SHARD, WIDE), jnp.bfloat16),
            pltpu.VMEM((ROWS, WIDE), jnp.bfloat16),
            pltpu.VMEM((ROWS, 128), jnp.float32),
            pltpu.VMEM((ROWS, 128), jnp.float32),
            pltpu.VMEM((ROWS, LATENT), jnp.float32),
            pltpu.VMEM((ROWS, LATENT), jnp.bfloat16),
            pltpu.VMEM((1024, 1024), jnp.bfloat16),
            pltpu.VMEM((8, TOK, 1024), jnp.bfloat16),
            pltpu.VMEM((8, TOK, 1024), jnp.bfloat16),
            pltpu.VMEM((4, 4, TOK, 512), jnp.bfloat16),
            pltpu.VMEM((4 * TOK, 512), jnp.bfloat16),
            pltpu.VMEM((4, 4 * TOK, 128), jnp.bfloat16),
            dma((5,)),
            dma((3,)),
            dma((32,)),
            dma((24,)),
            dma((16,)),
            dma((8,)),
            dma((6,)),
            dma((4,)),
            dma((16,)),
            dma((16,)),
            dma((16,)),
            dma((32,)),
            dma((32,)),
            dma((8,)),
            dma((8,)),
            dma((8,)),
            dma((16,)),
            dma((16,)),
            dma((16,)),
        ],
        compiler_params=pltpu.CompilerParams(
            collective_id=0, has_side_effects=True, vmem_limit_bytes=63 << 20
        ),
        cost_estimate=pl.CostEstimate(
            flops=8_000_000_000, bytes_accessed=4_000_000, transcendentals=2_600_000
        ),
        name="mla_prefill",
    )(span_query, span_latent, cache_latent, cache_length, kv_up_weight, out_weight.T)


def solution(mesh):
    return jax.shard_map(
        on_device,
        mesh=mesh,
        in_specs=(
            P("ctx", "head"),
            P("ctx", None),
            P("ctx", None),
            P(),
            P(None, "head"),
            P("head", "ctx"),
        ),
        out_specs=P("head", "ctx"),
        check_vma=False,
    )
```

```python
import functools
import math

import jax
import jax.numpy as jnp
from jax import lax
from jax.experimental import pallas as pl
from jax.experimental.pallas import tpu as pltpu
from jax.sharding import PartitionSpec as P

LATENT = 512
ROPE = 64
NOPE = 128
VDIM = 128
HEADS = 8
TOK = 64
CROWS = 16
SHARD = TOK + CROWS
WIDE = 640
HALF = 4 * SHARD
BLOCK = 2 * HALF
COLS = 112
ROWS = HEADS * TOK
MASKED = -1e30
FAR = 1 << 30
MESH = pl.DeviceIdType.MESH
SCALE2 = (1.0 + 0.1 * math.log(40.0)) ** 2 / math.sqrt(NOPE + ROPE) * math.log2(math.e)


def kernel(
    query_hbm,
    span_hbm,
    cache_hbm,
    length_ref,
    kv_hbm,
    w_hbm,
    out_ref,
    query_ref,
    span_ref,
    cache_ref,
    kv_ref,
    keys,
    mine,
    queries,
    maxima,
    totals,
    acc,
    latent_out,
    wbuf,
    att,
    part,
    landed,
    reduced,
    s_in,
    s_pre,
    s_ring,
    s_leaf,
    s_far,
    s_sib,
    s_w,
    s_wsib,
    s_att,
    s_x,
    s_f,
    r_ring,
    r_leaf,
    r_sib,
    r_w,
    r_att,
    r_x,
    r_f,
):
    ctx = lax.axis_index("ctx")
    head = lax.axis_index("head")
    x, yh = (head & 3), (head >> 2)
    q, z, c = (ctx >> 4), (((ctx >> 1)) & 7), (ctx & 1)
    y = yh * 4 + q

    def device(dx, dy, dz, dc):
        return {"ctx": (((dy & 3)) * 8 + dz) * 2 + dc, "head": ((dy >> 2)) * 4 + dx}

    z_up = device(x, y, ((z + 1) & 7), c)
    z_down = device(x, y, ((z + 7) & 7), c)
    z_up2 = device(x, y, ((z + 2) & 7), c)
    z_down2 = device(x, y, ((z + 6) & 7), c)
    sibling = device(x, y, z, 1 - c)
    lead = jnp.where(c == 0, x, q)

    def leaf(delta):
        step = 1 if delta == 1 else 7
        return device(
            jnp.where(c == 0, ((x + delta) & 3), x), jnp.where(c == 0, y, ((y + step) & 7)), z, c
        )

    x0 = 2 * ((q & 1))
    role = ((x - x0 + 4) & 3)
    my_j = jnp.where((role == 1) | (role == 2), 1, 0)
    my_pair = (role >> 1)

    def target(b):
        return x0 + my_j, 4 * ((q >> 1)) + 2 * my_pair + (b >> 1), (b & 1)

    def is_me(dx, dy, dc):
        return (dx == x) & (dy == y) & (dc == c)

    def copy(src, dst, ssem, rsem, dev):
        return pltpu.make_async_remote_copy(
            src_ref=src, dst_ref=dst, send_sem=ssem, recv_sem=rsem, device_id=dev, device_id_type=MESH
        )

    def w_rows(qp, core):
        return wbuf.at[pl.ds(pl.multiple_of(qp * 256 + core * 128, 128), COLS)]

    loads = [
        pltpu.make_async_copy(src, dst, s_in.at[n])
        for n, (src, dst) in enumerate(
            (
                (span_hbm, span_ref),
                (cache_hbm, cache_ref),
                (query_hbm, query_ref),
                (kv_hbm, kv_ref),
                (w_hbm, w_rows(q, c)),
            )
        )
    ]
    barrier = pltpu.get_barrier_semaphore()

    def greet(dev):
        pl.semaphore_signal(barrier, inc=1, device_id=dev, device_id_type=MESH)

    for dev in (z_up, z_down, z_up2, z_down2):
        greet(dev)
    greet(sibling)
    for d in (1, 2, 3):
        greet(device(((x + d) & 3), y, z, c))
    for d in (1, 2, 6, 7):
        greet(device(x, ((y + d) & 7), z, c))
    src_q = 2 * yh + (x >> 1)
    src_j = (x & 1)
    src_x = jnp.where((q >> 1) == 0, x, ((2 * ((x >> 1)) + 3 - src_j) & 3))
    for b in range(4):
        sx, sy, sc = src_x, src_q + 4 * ((b >> 1)), (b & 1)

        @pl.when(jnp.logical_not(is_me(sx, sy, sc)))
        def _():
            greet(device(sx, sy, z, sc))

    for load in loads:
        load.start()

    selfs = 0
    for b in range(4):
        selfs = selfs + jnp.where(is_me(*target(b)), 1, 0)

    for n in range(8):
        wbuf[n * 128 + COLS : (n + 1) * 128] = jnp.zeros((128 - COLS, 1024), jnp.bfloat16)
    loads[0].wait()
    loads[1].wait()

    mine[:CROWS, :LATENT] = cache_ref[:, :LATENT]
    mine[CROWS:, :LATENT] = span_ref[:, :LATENT]
    mine[:CROWS, LATENT:] = jnp.concatenate(
        [cache_ref[:, LATENT:], jnp.zeros((CROWS, 64), jnp.bfloat16)], axis=1
    )
    mine[CROWS:, LATENT:] = jnp.concatenate(
        [span_ref[:, LATENT:], jnp.zeros((TOK, 64), jnp.bfloat16)], axis=1
    )

    def slot(zp, qp):
        return keys.at[zp, pl.ds(pl.multiple_of(c * HALF + qp * SHARD, SHARD), SHARD)]

    has_primary = (c == 1) | (q == x)

    @pl.when(has_primary)
    def _():
        slot(z, lead)[...] = mine[...]

    pl.semaphore_wait(barrier, 4 + 1 + 3 + 4 + 4 - selfs)

    def at(k):
        return (z + 8 + jnp.where((k & 1) == 1, -(((k + 1) >> 1)), (k >> 1))) % 8

    parts = ((0, 48), (48, 32))

    def piece_of(zp, qp, n):
        start, rows = parts[n]
        return keys.at[zp, pl.ds(pl.multiple_of(c * HALF + qp * SHARD, SHARD) + start, rows)]

    def pre(m, n):
        d = (1, 7, 2)[m]
        start, rows = parts[n]
        src = mine.at[pl.ds(start, rows)]
        dev = device(x, ((y + d) & 7), z, c)
        return copy(src, piece_of(z, x, n), s_pre.at[2 * m + n], r_ring.at[2 * z + n], dev)

    sends_pre = (c == 0) & (q == x)

    @pl.when(sends_pre)
    def _():
        for n in range(2):
            for m in range(3):
                pre(m, n).start()

    def ring_copy(k, n, sem, dev):
        piece = piece_of(at(k), lead, n)
        return copy(piece, piece, s_ring.at[sem], r_ring.at[2 * at(k) + n], dev)

    def leaf_copy(k, n, m):
        piece = piece_of(at(k), lead, n)
        d = (1, 3)[m]
        sem = r_leaf.at[(at(k) * 4 + lead) * 2 + n]
        return copy(piece, piece, s_leaf.at[4 * k + 2 * n + m], sem, leaf(d))

    def leaf_wait(k, d, n):
        qp = (lead + d) & 3
        piece = piece_of(at(k), qp, n)
        copy(piece, piece, s_leaf.at[0], r_leaf.at[(at(k) * 4 + qp) * 2 + n], sibling).wait_recv()
        return qp

    def leaves(k, n):
        for m in range(2):
            leaf_copy(k, n, m).start()

    def first(n):
        ring_copy(0, n, n, z_up).start()
        ring_copy(0, n, 10 + n, z_down).start()
        leaves(0, n)

    def stage1(k, n):
        ring_copy(k, n, 0, z_up).wait_recv()

        @pl.when((k == 1) | (k == 3))
        def _():
            ring_copy(k, n, 2 * k + n, z_up).start()

        @pl.when((k == 2) | (k == 4))
        def _():
            ring_copy(k, n, 2 * k + n, z_down).start()

        @pl.when(k == 3 + n)
        def _():
            ring_copy(k, n, 12 + n, (z_up2, z_down2)[n]).start()

        leaves(k, n)

    def half(zp, core):
        return keys.at[zp, pl.ds(pl.multiple_of(core * HALF, HALF), HALF)]

    def sib_copy(k):
        zp = at(k)
        return copy(half(zp, c), half(zp, c), s_sib.at[k], r_sib.at[zp], sibling)

    def pass_copy(k, n, qp):
        piece = piece_of(at(k), qp, n)
        sem = r_leaf.at[(at(k) * 4 + qp) * 2 + n]
        return copy(piece, piece, s_far.at[2 * k + n], sem, leaf((3, 1)[n]))

    def stage2(k):
        for n, d in enumerate((1, 3)):
            pass_copy(k, n, leaf_wait(k, d, n)).start()

    def stage3(k):
        for n, d in enumerate((3, 1)):
            leaf_wait(k, d, n)
            leaf_wait(k, 2, n)
        sib_copy(k).start()

    place = lax.broadcasted_iota(jnp.int32, (1, BLOCK), 1)
    core_of = jnp.where(place >= HALF, 1, 0)
    within = place - core_of * HALF
    plane = sum(jnp.where(within >= n * SHARD, 1, 0) for n in (1, 2, 3))
    row = within - plane * SHARD
    token_base = plane * 1024 + core_of * TOK + row - CROWS
    cache_base = plane * 256 + core_of * CROWS + row
    cached = row < CROWS
    length = length_ref[0]

    def flash(zs, start, count):
        rows = pl.ds(start, count)
        token = ctx * TOK + (lax.broadcasted_iota(jnp.int32, (count, 1), 0) & (TOK - 1))
        scores = []
        for zp in zs:
            code = jnp.where(
                cached,
                jnp.where(cache_base + zp * 32 < length, -1, FAR),
                token_base + zp * 128,
            )
            product = lax.dot_general(
                queries[rows], keys[zp], (((1,), (1,)), ((), ())), preferred_element_type=jnp.float32
            )
            scores.append(jnp.where(code <= token, product * SCALE2, MASKED))
        before = maxima[rows, :1]
        raised = before
        for part_scores in scores:
            raised = jnp.maximum(raised, jnp.max(part_scores, axis=1, keepdims=True))
        factor = jnp.exp2(before - raised)
        maxima[rows] = jnp.broadcast_to(raised, (count, 128))
        total = totals[rows] * factor
        value = acc[rows] * factor
        for zp, part_scores in zip(zs, scores):
            weights = jnp.exp2(part_scores - raised)
            total = total + jnp.sum(weights, axis=1, keepdims=True)
            value = value + jnp.dot(
                weights.astype(jnp.bfloat16), keys[zp, :, :LATENT], preferred_element_type=jnp.float32
            )
        totals[rows] = total
        acc[rows] = value

    for n in range(2):

        @pl.when(jnp.logical_not(has_primary))
        def _():
            pre(0, n).wait_recv()

        first(n)


    def w_move(qp, sem, dev):
        return copy(w_rows(qp, c), w_rows(qp, c), s_w.at[sem], r_w.at[qp * 2 + c], dev)

    def w_sib(qp):
        return copy(w_rows(qp, c), w_rows(qp, c), s_wsib.at[qp], r_w.at[qp * 2 + c], sibling)

    def w_wait(qp, core):
        copy(w_rows(qp, core), w_rows(qp, core), s_w.at[0], r_w.at[qp * 2 + core], sibling).wait_recv()

    y_up = device(x, ((y + 1) & 7), z, c)
    y_down = device(x, ((y + 7) & 7), z, c)

    def w_round(n):
        @pl.when(q >= n)
        def _():
            if n > 0:
                w_wait(q - n, c)
                w_sib(q - n).start()

            @pl.when(q < 3)
            def _():
                w_move(q - n, n, y_up).start()

        @pl.when(q + n < 4)
        def _():
            if n > 0:
                w_wait(q + n, c)
                w_sib(q + n).start()

            @pl.when(q > 0)
            def _():
                w_move(q + n, 3 + n, y_down).start()

    loads[4].wait()
    w_round(0)
    w_sib(q).start()
    loads[2].wait()
    loads[3].wait()

    for h in range(HEADS):
        nope = query_ref[:, h * 192 : h * 192 + NOPE]
        rope = query_ref[:, h * 192 + NOPE : (h + 1) * 192]
        absorbed = lax.dot_general(
            nope,
            kv_ref[:, h * 256 : h * 256 + NOPE],
            (((1,), (1,)), ((), ())),
            preferred_element_type=jnp.float32,
        ).astype(jnp.bfloat16)
        queries[h * TOK : (h + 1) * TOK, :LATENT] = absorbed
        queries[h * TOK : (h + 1) * TOK, LATENT:] = jnp.concatenate(
            [rope, jnp.zeros((TOK, 64), jnp.bfloat16)], axis=1
        )
    maxima[...] = jnp.full((ROWS, 128), MASKED, jnp.float32)
    totals[...] = jnp.zeros((ROWS, 128), jnp.float32)
    acc[...] = jnp.zeros((ROWS, LATENT), jnp.float32)

    def pair_of(g, stage):
        for k in (2 * g - 1, 2 * g):

            @pl.when((k >= 0) & (k < 8))
            def _():
                stage(k)

    def attend(g):
        @pl.when(g == 0)
        def _():
            sib_copy(0).wait_recv()
            flash([z], 0, ROWS)

        @pl.when(g > 0)
        def _():
            ks = (2 * g - 1, 2 * g)
            for k in ks:
                sib_copy(k).wait_recv()
            flash([at(k) for k in ks], 0, ROWS)

    def w_last():
        @pl.when(q == 3)
        def _():
            w_wait(0, c)
            w_sib(0).start()

        @pl.when(q == 0)
        def _():
            w_wait(3, c)
            w_sib(3).start()

    def body(j, carry):
        @pl.when(j < 4)
        def _():
            for n in range(2):
                pair_of(j + 1, functools.partial(stage1, n=n))

        @pl.when(j < 5)
        def _():
            pair_of(j, stage2)

        @pl.when(j > 0)
        def _():
            pair_of(j - 1, stage3)

        @pl.when(j == 1)
        def _():
            w_round(1)

        @pl.when(j == 3)
        def _():
            w_round(2)

        @pl.when(j == 5)
        def _():
            w_last()

        @pl.when(j > 1)
        def _():
            attend(j - 2)

        return carry

    lax.fori_loop(0, 6, body, 0)

    def att_copy(k, n, sem, dev):
        piece = att.at[at(k), :, pl.ds(n * 256, 256)]
        return copy(piece, piece, s_att.at[sem], r_att.at[at(k) * 4 + n], dev)

    sib_copy(7).wait_recv()
    for hf in (0, 1):
        rows = pl.ds(hf * 256, 256)
        flash([at(7)], hf * 256, 256)
        latent_out[rows] = (acc[rows] / totals[rows, :1]).astype(jnp.bfloat16)
        for h in range(4 * hf, 4 * hf + 4):
            att[z, :, h * VDIM : (h + 1) * VDIM] = jnp.dot(
                latent_out[h * TOK : (h + 1) * TOK],
                kv_ref[:, h * 256 + NOPE : (h + 1) * 256],
                preferred_element_type=jnp.float32,
            ).astype(jnp.bfloat16)
        for n in (2 * hf, 2 * hf + 1):
            att_copy(0, n, n, z_up).start()
            att_copy(0, n, 4 + n, z_down).start()

    for qp in range(4):
        w_wait(qp, 1 - c)

    def collector(zp, pair):
        j = (zp >> 2)
        return ((x0 + jnp.where(pair == 0, j, 3 - j)) & 3)

    def x_copy(zp, pair):
        r = collector(zp, pair)
        return r, copy(
            part.at[zp, :, pl.ds(pair * 512, 512)],
            landed.at[x, (zp & 3)],
            s_x.at[zp * 2 + pair],
            r_x.at[x * 4 + (zp & 3)],
            device(r, y, z, c),
        )

    def project(zs):
        rows = jnp.concatenate([att[zp] for zp in zs], axis=0)
        product = lax.dot_general(
            rows, wbuf[...], (((1,), (1,)), ((), ())), preferred_element_type=jnp.float32
        ).astype(jnp.bfloat16)
        for n, zp in enumerate(zs):
            part[zp] = product[n * TOK : (n + 1) * TOK]
            for pair in (0, 1):
                r, cp = x_copy(zp, pair)

                @pl.when(r != x)
                def _():
                    cp.start()

    me_slot = yh * 2 + c

    def final_parts(b, zi):
        rows = pl.ds(pl.multiple_of(zi * TOK, TOK), TOK)
        there = pl.ds(pl.multiple_of(zi * 128 + c * TOK, TOK), TOK)
        return reduced.at[rows, pl.ds(b * 128, 128)], out_ref.at[yh, there]

    def final_copy(b, zi):
        dx, dy, dc = target(b)
        src, dst = final_parts(b, zi)
        return copy(src, dst, s_f.at[b * 4 + zi], r_f.at[me_slot * 4 + zi], device(dx, dy, z, dc))

    def reduce(k):
        zp = at(k)
        zi = (zp & 3)

        @pl.when((zp >> 2) == my_j)
        def _():
            lanes = pl.ds(pl.multiple_of(my_pair * 512, 512), 512)
            total = part[zp, :, lanes].astype(jnp.float32)
            for d in (1, 2, 3):
                xs = ((x + d) & 3)
                copy(landed.at[xs, zi], landed.at[xs, zi], s_x.at[0], r_x.at[xs * 4 + zi], sibling).wait_recv()
                total = total + landed[xs, zi].astype(jnp.float32)
            reduced[pl.ds(pl.multiple_of(zi * TOK, TOK), TOK)] = total.astype(jnp.bfloat16)
            for b in range(4):
                here = is_me(*target(b))

                @pl.when(here)
                def _():
                    src, dst = final_parts(b, zi)
                    pltpu.make_async_copy(src, dst, r_f.at[me_slot * 4 + zi]).start()

                @pl.when(jnp.logical_not(here))
                def _():
                    final_copy(b, zi).start()

    project([z])

    def arrive(k):
        for n in range(4):
            att_copy(k, n, 0, z_up).wait_recv()

            @pl.when((k == 1) | (k == 3))
            def _():
                att_copy(k, n, 4 * k + 4 + n, z_up).start()

            @pl.when((k == 2) | (k == 4))
            def _():
                att_copy(k, n, 4 * k + 4 + n, z_down).start()

            if n < 2:

                @pl.when(k == 3)
                def _():
                    att_copy(k, n, 24 + n, z_up2).start()

            else:

                @pl.when(k == 4)
                def _():
                    att_copy(k, n, 24 + n, z_down2).start()

    def out_step(j, carry):
        ks = (2 * j - 1, 2 * j)
        for k in ks:
            arrive(k)
        project([at(k) for k in ks])
        reduce(2 * j - 2)

        @pl.when(j > 1)
        def _():
            reduce(2 * j - 3)

        return carry

    lax.fori_loop(1, 4, out_step, 0)
    arrive(7)
    project([at(7)])
    for k in (5, 6, 7):
        reduce(k)

    for n in range(4):
        for zi in range(4):
            dst = out_ref.at[n // 2, pl.ds(zi * 128 + (n % 2) * TOK, TOK)]
            copy(dst, dst, s_f.at[0], r_f.at[n * 4 + zi], sibling).wait_recv()

    @pl.when(sends_pre)
    def _():
        for n in range(2):
            for m in range(3):
                pre(m, n).wait_send()

    for sem in range(14):
        ring_copy(0, sem & 1, sem, z_up).wait_send()
    for k in range(8):
        for n in range(2):
            pass_copy(k, n, lead).wait_send()
            for m in range(2):
                leaf_copy(k, n, m).wait_send()
    for k in range(8):
        sib_copy(k).wait_send()
    for n in range(3):

        @pl.when((q >= n) & (q < 3))
        def _():
            w_move(0, n, y_up).wait_send()

        @pl.when((q + n < 4) & (q > 0))
        def _():
            w_move(0, 3 + n, y_down).wait_send()

    for qp in range(4):
        w_sib(qp).wait_send()
    for n in range(28):
        att_copy(0, 0, n, z_up).wait_send()
    for zp in range(8):
        for pair in (0, 1):
            r, cp = x_copy(zp, pair)

            @pl.when(r != x)
            def _():
                cp.wait_send()

    for b in range(4):

        @pl.when(jnp.logical_not(is_me(*target(b))))
        def _():
            for zi in range(4):
                final_copy(b, zi).wait_send()


def on_device(span_query, span_latent, cache_latent, cache_length, kv_up_weight, out_weight):
    hbm = pl.BlockSpec(memory_space=pltpu.HBM)
    dma = pltpu.SemaphoreType.DMA
    halves = pl.pallas_call(
        kernel,
        out_shape=jax.ShapeDtypeStruct((2, 512, 128), jnp.bfloat16),
        in_specs=[hbm, hbm, hbm, pl.BlockSpec(memory_space=pltpu.SMEM), hbm, hbm],
        out_specs=hbm,
        scratch_shapes=[
            pltpu.VMEM((TOK, HEADS * 192), jnp.bfloat16),
            pltpu.VMEM((TOK, LATENT + ROPE), jnp.bfloat16),
            pltpu.VMEM((CROWS, LATENT + ROPE), jnp.bfloat16),
            pltpu.VMEM((LATENT, HEADS * 256), jnp.bfloat16),
            pltpu.VMEM((8, BLOCK, WIDE), jnp.bfloat16),
            pltpu.VMEM((SHARD, WIDE), jnp.bfloat16),
            pltpu.VMEM((ROWS, WIDE), jnp.bfloat16),
            pltpu.VMEM((ROWS, 128), jnp.float32),
            pltpu.VMEM((ROWS, 128), jnp.float32),
            pltpu.VMEM((ROWS, LATENT), jnp.float32),
            pltpu.VMEM((ROWS, LATENT), jnp.bfloat16),
            pltpu.VMEM((1024, 1024), jnp.bfloat16),
            pltpu.VMEM((8, TOK, 1024), jnp.bfloat16),
            pltpu.VMEM((8, TOK, 1024), jnp.bfloat16),
            pltpu.VMEM((4, 4, TOK, 512), jnp.bfloat16),
            pltpu.VMEM((4 * TOK, 512), jnp.bfloat16),
            dma((5,)),
            dma((6,)),
            dma((14,)),
            dma((32,)),
            dma((16,)),
            dma((8,)),
            dma((6,)),
            dma((4,)),
            dma((28,)),
            dma((16,)),
            dma((16,)),
            dma((16,)),
            dma((64,)),
            dma((8,)),
            dma((8,)),
            dma((32,)),
            dma((16,)),
            dma((16,)),
        ],
        compiler_params=pltpu.CompilerParams(
            collective_id=0, has_side_effects=True, vmem_limit_bytes=63 << 20
        ),
        cost_estimate=pl.CostEstimate(
            flops=8_000_000_000, bytes_accessed=4_000_000, transcendentals=2_600_000
        ),
        name="mla_prefill",
    )(span_query, span_latent, cache_latent, cache_length, kv_up_weight, out_weight.T)
    total = halves[0].astype(jnp.float32) + halves[1].astype(jnp.float32)
    return total[:, :COLS].astype(jnp.bfloat16)


def solution(mesh):
    return jax.shard_map(
        on_device,
        mesh=mesh,
        in_specs=(
            P("ctx", "head"),
            P("ctx", None),
            P("ctx", None),
            P(),
            P(None, "head"),
            P("head", "ctx"),
        ),
        out_specs=P("head", "ctx"),
        check_vma=False,
    )
```

```python
import functools
import math

import jax
import jax.numpy as jnp
from jax import lax
from jax.experimental import pallas as pl
from jax.experimental.pallas import tpu as pltpu
from jax.sharding import PartitionSpec as P

LATENT = 512
ROPE = 64
NOPE = 128
VDIM = 128
HEADS = 8
TOK = 64
CROWS = 16
SHARD = TOK + CROWS
WIDE = 640
HALF = 4 * SHARD
BLOCK = 2 * HALF
COLS = 112
ROWS = HEADS * TOK
MASKED = -1e30
FAR = 1 << 30
MESH = pl.DeviceIdType.MESH
SCALE2 = (1.0 + 0.1 * math.log(40.0)) ** 2 / math.sqrt(NOPE + ROPE) * math.log2(math.e)


def kernel(
    query_hbm,
    span_hbm,
    cache_hbm,
    length_ref,
    kv_hbm,
    w_hbm,
    out_ref,
    query_ref,
    span_ref,
    cache_ref,
    kv_ref,
    keys,
    mine,
    queries,
    maxima,
    totals,
    acc,
    latent_out,
    wbuf,
    att,
    part,
    landed,
    reduced,
    s_in,
    s_pre,
    s_ring,
    s_leaf,
    s_far,
    s_sib,
    s_w,
    s_wsib,
    s_att,
    s_x,
    s_f,
    r_ring,
    r_leaf,
    r_sib,
    r_w,
    r_att,
    r_x,
    r_f,
):
    ctx = lax.axis_index("ctx")
    head = lax.axis_index("head")
    x, yh = (head & 3), (head >> 2)
    q, z, c = (ctx >> 4), (((ctx >> 1)) & 7), (ctx & 1)
    y = yh * 4 + q

    def device(dx, dy, dz, dc):
        return {"ctx": (((dy & 3)) * 8 + dz) * 2 + dc, "head": ((dy >> 2)) * 4 + dx}

    z_up = device(x, y, ((z + 1) & 7), c)
    z_down = device(x, y, ((z + 7) & 7), c)
    z_up2 = device(x, y, ((z + 2) & 7), c)
    z_down2 = device(x, y, ((z + 6) & 7), c)
    sibling = device(x, y, z, 1 - c)
    lead = jnp.where(c == 0, x, q)

    def leaf(delta):
        step = 1 if delta == 1 else 7
        return device(
            jnp.where(c == 0, ((x + delta) & 3), x), jnp.where(c == 0, y, ((y + step) & 7)), z, c
        )

    x0 = 2 * ((q & 1))
    role = ((x - x0 + 4) & 3)
    my_j = jnp.where((role == 1) | (role == 2), 1, 0)
    my_pair = (role >> 1)

    def target(b):
        return x0 + my_j, 4 * ((q >> 1)) + 2 * my_pair + (b >> 1), (b & 1)

    def is_me(dx, dy, dc):
        return (dx == x) & (dy == y) & (dc == c)

    def copy(src, dst, ssem, rsem, dev):
        return pltpu.make_async_remote_copy(
            src_ref=src, dst_ref=dst, send_sem=ssem, recv_sem=rsem, device_id=dev, device_id_type=MESH
        )

    def w_rows(qp, core):
        return wbuf.at[pl.ds(pl.multiple_of(qp * 256 + core * 128, 128), COLS)]

    loads = [
        pltpu.make_async_copy(src, dst, s_in.at[n])
        for n, (src, dst) in enumerate(
            (
                (span_hbm, span_ref),
                (cache_hbm, cache_ref),
                (query_hbm, query_ref),
                (kv_hbm, kv_ref),
                (w_hbm, w_rows(q, c)),
            )
        )
    ]
    barrier = pltpu.get_barrier_semaphore()

    def greet(dev):
        pl.semaphore_signal(barrier, inc=1, device_id=dev, device_id_type=MESH)

    for dev in (z_up, z_down, z_up2, z_down2):
        greet(dev)
    greet(sibling)
    for d in (1, 2, 3):
        greet(device(((x + d) & 3), y, z, c))
    for d in (1, 2, 6, 7):
        greet(device(x, ((y + d) & 7), z, c))
    src_q = 2 * yh + (x >> 1)
    src_j = (x & 1)
    src_x = jnp.where((q >> 1) == 0, x, ((2 * ((x >> 1)) + 3 - src_j) & 3))
    for b in range(4):
        sx, sy, sc = src_x, src_q + 4 * ((b >> 1)), (b & 1)

        @pl.when(jnp.logical_not(is_me(sx, sy, sc)))
        def _():
            greet(device(sx, sy, z, sc))

    for load in loads:
        load.start()

    selfs = 0
    for b in range(4):
        selfs = selfs + jnp.where(is_me(*target(b)), 1, 0)

    for n in range(8):
        wbuf[n * 128 + COLS : (n + 1) * 128] = jnp.zeros((128 - COLS, 1024), jnp.bfloat16)
    loads[0].wait()
    loads[1].wait()

    mine[:CROWS, :LATENT] = cache_ref[:, :LATENT]
    mine[CROWS:, :LATENT] = span_ref[:, :LATENT]
    mine[:CROWS, LATENT:] = jnp.concatenate(
        [cache_ref[:, LATENT:], jnp.zeros((CROWS, 64), jnp.bfloat16)], axis=1
    )
    mine[CROWS:, LATENT:] = jnp.concatenate(
        [span_ref[:, LATENT:], jnp.zeros((TOK, 64), jnp.bfloat16)], axis=1
    )

    def slot(zp, qp):
        return keys.at[zp, pl.ds(pl.multiple_of(c * HALF + qp * SHARD, SHARD), SHARD)]

    has_primary = (c == 1) | (q == x)

    @pl.when(has_primary)
    def _():
        slot(z, lead)[...] = mine[...]

    pl.semaphore_wait(barrier, 4 + 1 + 3 + 4 + 4 - selfs)

    def at(k):
        return (z + 8 + jnp.where((k & 1) == 1, -(((k + 1) >> 1)), (k >> 1))) % 8

    parts = ((0, 48), (48, 32))

    def piece_of(zp, qp, n):
        start, rows = parts[n]
        return keys.at[zp, pl.ds(pl.multiple_of(c * HALF + qp * SHARD, SHARD) + start, rows)]

    def pre(m, n):
        d = (1, 7, 2)[m]
        start, rows = parts[n]
        src = mine.at[pl.ds(start, rows)]
        dev = device(x, ((y + d) & 7), z, c)
        return copy(src, piece_of(z, x, n), s_pre.at[2 * m + n], r_ring.at[2 * z + n], dev)

    sends_pre = (c == 0) & (q == x)

    @pl.when(sends_pre)
    def _():
        for n in range(2):
            for m in range(3):
                pre(m, n).start()

    def ring_copy(k, n, sem, dev):
        piece = piece_of(at(k), lead, n)
        return copy(piece, piece, s_ring.at[sem], r_ring.at[2 * at(k) + n], dev)

    def leaf_copy(k, n, m):
        piece = piece_of(at(k), lead, n)
        d = (1, 3)[m]
        sem = r_leaf.at[(at(k) * 4 + lead) * 2 + n]
        return copy(piece, piece, s_leaf.at[4 * k + 2 * n + m], sem, leaf(d))

    def leaf_wait(k, d, n):
        qp = (lead + d) & 3
        piece = piece_of(at(k), qp, n)
        copy(piece, piece, s_leaf.at[0], r_leaf.at[(at(k) * 4 + qp) * 2 + n], sibling).wait_recv()
        return qp

    def leaves(k, n):
        for m in range(2):
            leaf_copy(k, n, m).start()

    def first(n):
        ring_copy(0, n, n, z_up).start()
        ring_copy(0, n, 10 + n, z_down).start()
        leaves(0, n)

    def stage1(k, n):
        ring_copy(k, n, 0, z_up).wait_recv()

        @pl.when((k == 1) | (k == 3))
        def _():
            ring_copy(k, n, 2 * k + n, z_up).start()

        @pl.when((k == 2) | (k == 4))
        def _():
            ring_copy(k, n, 2 * k + n, z_down).start()

        @pl.when(k == 3 + n)
        def _():
            ring_copy(k, n, 12 + n, (z_up2, z_down2)[n]).start()

        leaves(k, n)

    def half(zp, core):
        return keys.at[zp, pl.ds(pl.multiple_of(core * HALF, HALF), HALF)]

    def sib_copy(k):
        zp = at(k)
        return copy(half(zp, c), half(zp, c), s_sib.at[k], r_sib.at[zp], sibling)

    def pass_copy(k, n, qp):
        piece = piece_of(at(k), qp, n)
        sem = r_leaf.at[(at(k) * 4 + qp) * 2 + n]
        return copy(piece, piece, s_far.at[2 * k + n], sem, leaf((3, 1)[n]))

    def stage2(k):
        for n, d in enumerate((1, 3)):
            pass_copy(k, n, leaf_wait(k, d, n)).start()

    def stage3(k):
        for n, d in enumerate((3, 1)):
            leaf_wait(k, d, n)
            leaf_wait(k, 2, n)
        sib_copy(k).start()

    place = lax.broadcasted_iota(jnp.int32, (1, BLOCK), 1)
    core_of = jnp.where(place >= HALF, 1, 0)
    within = place - core_of * HALF
    plane = sum(jnp.where(within >= n * SHARD, 1, 0) for n in (1, 2, 3))
    row = within - plane * SHARD
    token_base = plane * 1024 + core_of * TOK + row - CROWS
    cache_base = plane * 256 + core_of * CROWS + row
    cached = row < CROWS
    length = length_ref[0]

    def flash(zs, start, count):
        halves = []
        for first_row in range(start, start + count, 256):
            rows = pl.ds(first_row, 256)
            token = ctx * TOK + (lax.broadcasted_iota(jnp.int32, (256, 1), 0) & (TOK - 1))
            scores = []
            for zp in zs:
                code = jnp.where(
                    cached,
                    jnp.where(cache_base + zp * 32 < length, -1, FAR),
                    token_base + zp * 128,
                )
                product = lax.dot_general(
                    queries[rows], keys[zp], (((1,), (1,)), ((), ())), preferred_element_type=jnp.float32
                )
                scores.append(jnp.where(code <= token, product * SCALE2, MASKED))
            halves.append((rows, scores))
        for rows, scores in halves:
            before = maxima[rows, :1]
            raised = before
            for part_scores in scores:
                raised = jnp.maximum(raised, jnp.max(part_scores, axis=1, keepdims=True))
            factor = jnp.exp2(before - raised)
            maxima[rows] = jnp.broadcast_to(raised, (256, 128))
            total = totals[rows] * factor
            value = acc[rows] * factor
            for zp, part_scores in zip(zs, scores):
                weights = jnp.exp2(part_scores - raised)
                total = total + jnp.sum(weights, axis=1, keepdims=True)
                value = value + jnp.dot(
                    weights.astype(jnp.bfloat16), keys[zp, :, :LATENT], preferred_element_type=jnp.float32
                )
            totals[rows] = total
            acc[rows] = value

    for n in range(2):

        @pl.when(jnp.logical_not(has_primary))
        def _():
            pre(0, n).wait_recv()

        first(n)


    def w_move(qp, sem, dev):
        return copy(w_rows(qp, c), w_rows(qp, c), s_w.at[sem], r_w.at[qp * 2 + c], dev)

    def w_sib(qp):
        return copy(w_rows(qp, c), w_rows(qp, c), s_wsib.at[qp], r_w.at[qp * 2 + c], sibling)

    def w_wait(qp, core):
        copy(w_rows(qp, core), w_rows(qp, core), s_w.at[0], r_w.at[qp * 2 + core], sibling).wait_recv()

    y_up = device(x, ((y + 1) & 7), z, c)
    y_down = device(x, ((y + 7) & 7), z, c)

    def w_round(n):
        @pl.when(q >= n)
        def _():
            if n > 0:
                w_wait(q - n, c)
                w_sib(q - n).start()

            @pl.when(q < 3)
            def _():
                w_move(q - n, n, y_up).start()

        @pl.when(q + n < 4)
        def _():
            if n > 0:
                w_wait(q + n, c)
                w_sib(q + n).start()

            @pl.when(q > 0)
            def _():
                w_move(q + n, 3 + n, y_down).start()

    loads[4].wait()
    w_round(0)
    w_sib(q).start()
    loads[2].wait()
    loads[3].wait()

    for h in range(HEADS):
        nope = query_ref[:, h * 192 : h * 192 + NOPE]
        rope = query_ref[:, h * 192 + NOPE : (h + 1) * 192]
        absorbed = lax.dot_general(
            nope,
            kv_ref[:, h * 256 : h * 256 + NOPE],
            (((1,), (1,)), ((), ())),
            preferred_element_type=jnp.float32,
        ).astype(jnp.bfloat16)
        queries[h * TOK : (h + 1) * TOK, :LATENT] = absorbed
        queries[h * TOK : (h + 1) * TOK, LATENT:] = jnp.concatenate(
            [rope, jnp.zeros((TOK, 64), jnp.bfloat16)], axis=1
        )
    maxima[...] = jnp.full((ROWS, 128), MASKED, jnp.float32)
    totals[...] = jnp.zeros((ROWS, 128), jnp.float32)
    acc[...] = jnp.zeros((ROWS, LATENT), jnp.float32)

    def pair_of(g, stage):
        for k in (2 * g - 1, 2 * g):

            @pl.when((k >= 0) & (k < 8))
            def _():
                stage(k)

    def attend(g):
        @pl.when(g == 0)
        def _():
            sib_copy(0).wait_recv()
            flash([z], 0, ROWS)

        @pl.when(g > 0)
        def _():
            ks = (2 * g - 1, 2 * g)
            for k in ks:
                sib_copy(k).wait_recv()
            flash([at(k) for k in ks], 0, ROWS)

    def w_last():
        @pl.when(q == 3)
        def _():
            w_wait(0, c)
            w_sib(0).start()

        @pl.when(q == 0)
        def _():
            w_wait(3, c)
            w_sib(3).start()

    def body(j, carry):
        @pl.when(j < 4)
        def _():
            for n in range(2):
                pair_of(j + 1, functools.partial(stage1, n=n))

        @pl.when(j < 5)
        def _():
            pair_of(j, stage2)

        @pl.when(j > 0)
        def _():
            pair_of(j - 1, stage3)

        @pl.when(j == 1)
        def _():
            w_round(1)

        @pl.when(j == 3)
        def _():
            w_round(2)

        @pl.when(j == 5)
        def _():
            w_last()

        @pl.when(j > 1)
        def _():
            attend(j - 2)

        return carry

    lax.fori_loop(0, 6, body, 0)

    def att_copy(k, n, sem, dev):
        piece = att.at[at(k), :, pl.ds(n * 256, 256)]
        return copy(piece, piece, s_att.at[sem], r_att.at[at(k) * 4 + n], dev)

    sib_copy(7).wait_recv()
    for hf in (0, 1):
        rows = pl.ds(hf * 256, 256)
        flash([at(7)], hf * 256, 256)
        latent_out[rows] = (acc[rows] / totals[rows, :1]).astype(jnp.bfloat16)
        for h in range(4 * hf, 4 * hf + 4):
            att[z, :, h * VDIM : (h + 1) * VDIM] = jnp.dot(
                latent_out[h * TOK : (h + 1) * TOK],
                kv_ref[:, h * 256 + NOPE : (h + 1) * 256],
                preferred_element_type=jnp.float32,
            ).astype(jnp.bfloat16)
        for n in (2 * hf, 2 * hf + 1):
            att_copy(0, n, n, z_up).start()
            att_copy(0, n, 4 + n, z_down).start()

    for qp in range(4):
        w_wait(qp, 1 - c)

    def collector(zp, pair):
        j = (zp >> 2)
        return ((x0 + jnp.where(pair == 0, j, 3 - j)) & 3)

    def x_copy(zp, pair):
        r = collector(zp, pair)
        return r, copy(
            part.at[zp, :, pl.ds(pair * 512, 512)],
            landed.at[x, (zp & 3)],
            s_x.at[zp * 2 + pair],
            r_x.at[x * 4 + (zp & 3)],
            device(r, y, z, c),
        )

    def project(zs):
        rows = jnp.concatenate([att[zp] for zp in zs], axis=0)
        product = lax.dot_general(
            rows, wbuf[...], (((1,), (1,)), ((), ())), preferred_element_type=jnp.float32
        ).astype(jnp.bfloat16)
        for n, zp in enumerate(zs):
            part[zp] = product[n * TOK : (n + 1) * TOK]
            for pair in (0, 1):
                r, cp = x_copy(zp, pair)

                @pl.when(r != x)
                def _():
                    cp.start()

    me_slot = yh * 2 + c

    def final_parts(b, zi):
        rows = pl.ds(pl.multiple_of(zi * TOK, TOK), TOK)
        there = pl.ds(pl.multiple_of(zi * 128 + c * TOK, TOK), TOK)
        return reduced.at[rows, pl.ds(b * 128, 128)], out_ref.at[yh, there]

    def final_copy(b, zi):
        dx, dy, dc = target(b)
        src, dst = final_parts(b, zi)
        return copy(src, dst, s_f.at[b * 4 + zi], r_f.at[me_slot * 4 + zi], device(dx, dy, z, dc))

    def reduce(k):
        zp = at(k)
        zi = (zp & 3)

        @pl.when((zp >> 2) == my_j)
        def _():
            lanes = pl.ds(pl.multiple_of(my_pair * 512, 512), 512)
            total = part[zp, :, lanes].astype(jnp.float32)
            for d in (1, 2, 3):
                xs = ((x + d) & 3)
                copy(landed.at[xs, zi], landed.at[xs, zi], s_x.at[0], r_x.at[xs * 4 + zi], sibling).wait_recv()
                total = total + landed[xs, zi].astype(jnp.float32)
            reduced[pl.ds(pl.multiple_of(zi * TOK, TOK), TOK)] = total.astype(jnp.bfloat16)
            for b in range(4):
                here = is_me(*target(b))

                @pl.when(here)
                def _():
                    src, dst = final_parts(b, zi)
                    pltpu.make_async_copy(src, dst, r_f.at[me_slot * 4 + zi]).start()

                @pl.when(jnp.logical_not(here))
                def _():
                    final_copy(b, zi).start()

    project([z])

    def arrive(k):
        for n in range(4):
            att_copy(k, n, 0, z_up).wait_recv()

            @pl.when((k == 1) | (k == 3))
            def _():
                att_copy(k, n, 4 * k + 4 + n, z_up).start()

            @pl.when((k == 2) | (k == 4))
            def _():
                att_copy(k, n, 4 * k + 4 + n, z_down).start()

            if n < 2:

                @pl.when(k == 3)
                def _():
                    att_copy(k, n, 24 + n, z_up2).start()

            else:

                @pl.when(k == 4)
                def _():
                    att_copy(k, n, 24 + n, z_down2).start()

    def out_step(j, carry):
        ks = (2 * j - 1, 2 * j)
        for k in ks:
            arrive(k)
        project([at(k) for k in ks])
        reduce(2 * j - 2)

        @pl.when(j > 1)
        def _():
            reduce(2 * j - 3)

        return carry

    lax.fori_loop(1, 4, out_step, 0)
    arrive(7)
    project([at(7)])
    for k in (5, 6, 7):
        reduce(k)

    for n in range(4):
        for zi in range(4):
            dst = out_ref.at[n // 2, pl.ds(zi * 128 + (n % 2) * TOK, TOK)]
            copy(dst, dst, s_f.at[0], r_f.at[n * 4 + zi], sibling).wait_recv()

    @pl.when(sends_pre)
    def _():
        for n in range(2):
            for m in range(3):
                pre(m, n).wait_send()

    for sem in range(14):
        ring_copy(0, sem & 1, sem, z_up).wait_send()
    for k in range(8):
        for n in range(2):
            pass_copy(k, n, lead).wait_send()
            for m in range(2):
                leaf_copy(k, n, m).wait_send()
    for k in range(8):
        sib_copy(k).wait_send()
    for n in range(3):

        @pl.when((q >= n) & (q < 3))
        def _():
            w_move(0, n, y_up).wait_send()

        @pl.when((q + n < 4) & (q > 0))
        def _():
            w_move(0, 3 + n, y_down).wait_send()

    for qp in range(4):
        w_sib(qp).wait_send()
    for n in range(28):
        att_copy(0, 0, n, z_up).wait_send()
    for zp in range(8):
        for pair in (0, 1):
            r, cp = x_copy(zp, pair)

            @pl.when(r != x)
            def _():
                cp.wait_send()

    for b in range(4):

        @pl.when(jnp.logical_not(is_me(*target(b))))
        def _():
            for zi in range(4):
                final_copy(b, zi).wait_send()


def on_device(span_query, span_latent, cache_latent, cache_length, kv_up_weight, out_weight):
    hbm = pl.BlockSpec(memory_space=pltpu.HBM)
    dma = pltpu.SemaphoreType.DMA
    halves = pl.pallas_call(
        kernel,
        out_shape=jax.ShapeDtypeStruct((2, 512, 128), jnp.bfloat16),
        in_specs=[hbm, hbm, hbm, pl.BlockSpec(memory_space=pltpu.SMEM), hbm, hbm],
        out_specs=hbm,
        scratch_shapes=[
            pltpu.VMEM((TOK, HEADS * 192), jnp.bfloat16),
            pltpu.VMEM((TOK, LATENT + ROPE), jnp.bfloat16),
            pltpu.VMEM((CROWS, LATENT + ROPE), jnp.bfloat16),
            pltpu.VMEM((LATENT, HEADS * 256), jnp.bfloat16),
            pltpu.VMEM((8, BLOCK, WIDE), jnp.bfloat16),
            pltpu.VMEM((SHARD, WIDE), jnp.bfloat16),
            pltpu.VMEM((ROWS, WIDE), jnp.bfloat16),
            pltpu.VMEM((ROWS, 128), jnp.float32),
            pltpu.VMEM((ROWS, 128), jnp.float32),
            pltpu.VMEM((ROWS, LATENT), jnp.float32),
            pltpu.VMEM((ROWS, LATENT), jnp.bfloat16),
            pltpu.VMEM((1024, 1024), jnp.bfloat16),
            pltpu.VMEM((8, TOK, 1024), jnp.bfloat16),
            pltpu.VMEM((8, TOK, 1024), jnp.bfloat16),
            pltpu.VMEM((4, 4, TOK, 512), jnp.bfloat16),
            pltpu.VMEM((4 * TOK, 512), jnp.bfloat16),
            dma((5,)),
            dma((6,)),
            dma((14,)),
            dma((32,)),
            dma((16,)),
            dma((8,)),
            dma((6,)),
            dma((4,)),
            dma((28,)),
            dma((16,)),
            dma((16,)),
            dma((16,)),
            dma((64,)),
            dma((8,)),
            dma((8,)),
            dma((32,)),
            dma((16,)),
            dma((16,)),
        ],
        compiler_params=pltpu.CompilerParams(
            collective_id=0, has_side_effects=True, vmem_limit_bytes=63 << 20
        ),
        cost_estimate=pl.CostEstimate(
            flops=8_000_000_000, bytes_accessed=4_000_000, transcendentals=2_600_000
        ),
        name="mla_prefill",
    )(span_query, span_latent, cache_latent, cache_length, kv_up_weight, out_weight.T)
    total = halves[0].astype(jnp.float32) + halves[1].astype(jnp.float32)
    return total[:, :COLS].astype(jnp.bfloat16)


def solution(mesh):
    return jax.shard_map(
        on_device,
        mesh=mesh,
        in_specs=(
            P("ctx", "head"),
            P("ctx", None),
            P("ctx", None),
            P(),
            P(None, "head"),
            P("head", "ctx"),
        ),
        out_specs=P("head", "ctx"),
        check_vma=False,
    )
```
